256 devices in a mesh: lat: 4 (over x_lo, core), lon: 64 (over y, x_hi, z).
Axes of the slice: x: 4 (x_hi: 2, x_lo: 2; x = x_hi * 2 + x_lo), y: 4, z: 8, core: 2. Of those that a mesh axis runs over, the one named last changes fastest.
Arguments:
- state: bfloat16 [64, 512, 256], P('lat', 'lon'), may hold values from -45 to 45
- cotangent: bfloat16 [64, 512, 256], P('lat', 'lon'), may hold values from -5 to 5
- land_sea: int32 [64, 512], P('lat', 'lon'), may hold values 0 or 1
- regime: int32 [4, 64, 16, 8, 1], P('lat', 'lon'), may hold values from 0 to 15; in each aligned block of 128 rows (0 to 127, 128 to 255, ..., all dimensions but the last counted through in order) at most 16 rows name the same one
- first_gain: float32 [256], replicated, may hold values from 0.1 to 1.9
- second_gain: float32 [256], replicated, may hold values from 0.1 to 1.9
- project_weight: bfloat16 [256, 768], replicated, may hold values from -0.375 to 0.375
- out_weight: bfloat16 [256, 256], replicated, may hold values from -0.375 to 0.375
- pos_bias: float32 [8, 49], replicated, may hold values from -3 to 315
- up_weight: bfloat16 [256, 16384], P(None, 'lon'), may hold values from -0.375 to 0.375
- down_weight: bfloat16 [16384, 256], P('lon'), may hold values from -0.1875 to 0.1875
Outputs:
- block_out: bfloat16 [64, 512, 256], P('lat', 'lon')
- grad_up: float32 [256, 16384], P(None, 'lon')
- grad_down: float32 [16384, 256], P('lon')
The draws below stay inside these ranges and needn't reach their ends.
Inputs may be any that keep to these rules, and one draw needn't show every extreme that they name: Among the 16 x 8 cells of one tile at most 16 share a regime, and some tile has exactly 16 cells of one regime. Every regime occurs somewhere.
All inputs are finite; a program needn't handle non-finite values. No bound on the sum of `land_sea` on one device may be relied on, other than what follows from the above.
Results may differ from the reference program's by a relative error of at most 0.022.
Values may be sent and summed in bfloat16 or wider, within the bound.
No kernel may reach another device: no remote copies, remote signals or barrier semaphores. Data moves between devices by JAX's collectives and lax.ppermute only.
A program may use at most 64 MiB of HBM per device.

```python
import math
import jax
import jax.numpy as jnp
import numpy as np
from jax import lax

D = 256
HEADS = 8
HD = 32
WINDOW = 7
EXPERTS = 16
FF = 1024
LAT_DEV = 16
LON_DEV = 8
CAP = 16
NLAT = 64
NLON = 512
N_LAT = 4
N_LON = 64


def draw_state(key, part):
    key = jax.random.fold_in(key, 11)
    normal_key, row_key, column_key = jax.random.split(key, 3)
    grid_shape = (NLAT, NLON, D)
    normal_part = jax.random.truncated_normal(normal_key, -3.0, 3.0, grid_shape, jnp.float32)
    row_scale = jnp.exp(jax.random.uniform(row_key, (NLAT, NLON, 1), jnp.float32, math.log(0.3), math.log(3.0)))
    column_scale = jnp.exp(jax.random.uniform(column_key, (1, 1, D), jnp.float32, math.log(0.3), math.log(3.0)))
    return (normal_part * row_scale * column_scale).astype(jnp.bfloat16)


def draw_pos_bias(key, part):
    key = jax.random.fold_in(key, 23)
    key_list = jax.random.split(key, 1)
    tap_count = WINDOW * WINDOW
    normal_part = jax.random.truncated_normal(key_list[0], -3.0, 3.0, (HEADS, tap_count), jnp.float32)
    return normal_part


def with_ends(result, stream_key, smallest, largest):
    extent = result.shape
    place = [jax.random.randint(jax.random.fold_in(stream_key, axis), (), 0, extent[axis]) for axis in range(len(extent))]
    result = result.at[tuple(place)].set(smallest)
    longest = extent.index(max(extent))
    place[longest] = (place[longest] + 1) % extent[longest]
    return result.at[tuple(place)].set(largest)


def shard_levels(rng, dims, shards, least, high):
    def one(axis_at, shards_of):
        draws = jax.random.uniform(jax.random.fold_in(jax.random.fold_in(rng, 6), axis_at), (shards_of,), jnp.float32, least / len(shards), high / len(shards))
        return jnp.repeat(jnp.exp(draws), dims[axis_at] // shards_of).reshape((-1,) + (1,) * (len(dims) - axis_at - 1))

    factor_of = one(*shards[0])
    for cut in shards[1:]:
        factor_of = factor_of * one(*cut)
    return factor_of


def deal_out(rng, own, number, rows, count, top, bound, skew):
    sequence = jax.random.permutation(rng, count)
    packed, usual = load_shares(count, rows * top, bound, skew, True), load_shares(count, rows * top, bound, skew, False)
    places = jnp.arange(count)

    def named(tallies, rotation):
        used = int((tallies > 0).sum())
        fixed = max(1, used // 4)
        moved = fixed + (places - fixed + rotation * (used - fixed)) % max(1, count - fixed)
        return jnp.zeros((count,), jnp.int32).at[sequence[jnp.where(places < fixed, places, moved)]].set(jnp.asarray(tallies, jnp.int32))

    tallies = jnp.where(number % 4 == 0, named(packed, number // 4), named(usual, number - number // 4 - 1))
    mixed = jax.random.permutation(jax.random.fold_in(own, 3), count)
    donor, sink = mixed[0:count // 2 * 2:2], mixed[1:count // 2 * 2:2]
    slack = jnp.minimum(tallies[donor] - 1, bound - tallies[sink]) // 2
    slack = jnp.where((donor == sequence[0]) | (sink == sequence[0]) | (tallies[sink] == 0), 0, jnp.maximum(slack, 0))
    moved = jax.random.randint(jax.random.fold_in(own, 4), (count // 2,), 0, 1 << 20) % (slack + 1)
    tallies = tallies.at[donor].add(-moved).at[sink].add(moved)
    items = jnp.searchsorted(jnp.cumsum(tallies), jnp.arange(rows * top), side="right").astype(jnp.int32)
    table = items.reshape(top, rows).T
    table = table[jax.random.permutation(jax.random.fold_in(own, 1), rows)]
    rotation = jax.random.randint(jax.random.fold_in(own, 2), (rows, 1), 0, top)
    return jnp.take_along_axis(table, (jnp.arange(top)[None, :] + rotation) % top, axis=1)


def load_shares(amount, total, limit, skew, full):
    weights = [(1 << 20) // math.isqrt(rank ** skew) + 1 for rank in range(1, amount + 1)]
    largest = limit if full else min(limit, max(-(-total // amount), total * weights[0] // sum(weights)))
    least = 1 if total - largest >= amount - 1 else 0
    given, surplus = [largest] + [least] * (amount - 1), total - largest - least * (amount - 1)
    while surplus > 0:
        movable = [i for i in range(1, amount) if given[i] < largest] or [i for i in range(1, amount) if given[i] < limit]
        whole, remaining = sum([weights[i] for i in movable]), surplus
        for i in movable:
            extra = min(limit - given[i], max(1, remaining * weights[i] // whole), surplus)
            given[i] = given[i] + extra
            surplus = surplus - extra
    return np.array(given)


def scatter_about(own_key, extent, scale, most, cuts=(), held_as=jnp.bfloat16):
    entries = scale * jax.random.normal(own_key, extent, jnp.float32)
    if cuts:
        entries = entries * shard_levels(own_key, extent, cuts, -0.22, 0.18)
    return jnp.clip(entries, -most, most).astype(held_as)


def setup_inputs(seed: int = 0) -> dict:
    streams_of = jax.random.split(jax.random.key(seed), 12)
    state = draw_state(jax.random.fold_in(streams_of[11], 71), 0)
    cotangent = scatter_about(streams_of[1], (NLAT, NLON, D), (64.0 / (NLAT * NLON) ** 0.5), 5.0, ((0, 4), (1, 64)))
    land_sea = with_ends((jax.random.randint(streams_of[2], (NLAT, NLON), 0, 10) < 7).astype(jnp.int32), jax.random.fold_in(streams_of[2], 1), 0, 1)
    regime_keys = jax.random.split(jax.random.fold_in(streams_of[3], 1), N_LAT * N_LON * LAT_DEV * LON_DEV // (LAT_DEV * LON_DEV))
    regime_turns = jax.random.permutation(jax.random.fold_in(streams_of[3], 3), N_LAT * N_LON * LAT_DEV * LON_DEV // (LAT_DEV * LON_DEV))
    regime = jax.vmap(lambda own, number: deal_out(jax.random.fold_in(streams_of[3], 2), own, number, LAT_DEV * LON_DEV, EXPERTS, 1, CAP, 2))(regime_keys, regime_turns).reshape((N_LAT, N_LON, LAT_DEV, LON_DEV, 1))
    first_gain = jnp.clip(1.0 + 0.18 * jax.random.normal(streams_of[4], (D,), jnp.float32), 0.1, 1.9)
    second_gain = jnp.clip(1.0 + 0.18 * jax.random.normal(streams_of[5], (D,), jnp.float32), 0.1, 1.9)
    project_weight = scatter_about(streams_of[6], (D, 3 * D), D ** -0.5, 0.375)
    out_weight = scatter_about(streams_of[7], (D, D), D ** -0.5, 0.375)
    pos_bias = draw_pos_bias(jax.random.fold_in(streams_of[11], 71), 0)
    up_weight = scatter_about(streams_of[9], (D, EXPERTS * FF), D ** -0.5, 0.375, ((1, 64),))
    down_weight = scatter_about(streams_of[10], (EXPERTS * FF, D), FF ** -0.5, 0.1875, ((0, 64),))
    return dict(state=state, cotangent=cotangent, land_sea=land_sea, regime=regime, first_gain=first_gain, second_gain=second_gain, project_weight=project_weight, out_weight=out_weight, pos_bias=pos_bias, up_weight=up_weight, down_weight=down_weight)


def layer_norm(values, gain_vec):
    values = values.astype(jnp.float32)
    mean_val = lax.optimization_barrier(jnp.mean(values, axis=-1, keepdims=True))
    spread = lax.optimization_barrier(jnp.mean(jnp.square(values - mean_val), axis=-1, keepdims=True))
    return ((values - mean_val) * lax.rsqrt(spread + 1e-05) * gain_vec).astype(jnp.bfloat16)

def gelu_value(inputs):
    return 0.5 * inputs * (1.0 + jax.scipy.special.erf(inputs * 0.7071067811865476))

def gelu_slope(inputs):
    return 0.5 * (1.0 + jax.scipy.special.erf(inputs * 0.7071067811865476)) + inputs * jnp.exp(-0.5 * inputs * inputs) * 0.3989422804014327

def reference(state, cotangent, land_sea, regime, first_gain, second_gain, project_weight, out_weight, pos_bias, up_weight, down_weight):
    cell_count = NLAT * NLON
    window_reach = WINDOW // 2
    center = WINDOW * WINDOW // 2
    score_scale = 1.0 / math.sqrt(HD)
    normed_in = layer_norm(state, first_gain).reshape(cell_count, D)
    triple = jnp.dot(normed_in, project_weight, preferred_element_type=jnp.float32).astype(jnp.bfloat16)
    queries = triple[:, :D].astype(jnp.float32).reshape(NLAT, NLON, HEADS, HD)
    lat_pad = ((window_reach, window_reach), (0, 0), (0, 0))
    key_rows = jnp.pad(triple[:, D:2 * D].reshape(NLAT, NLON, D), lat_pad)
    value_rows = jnp.pad(triple[:, 2 * D:].reshape(NLAT, NLON, D), lat_pad)
    mask_rows = jnp.pad(land_sea, ((window_reach, window_reach), (0, 0)))
    score_list = []
    valid_list = []
    for row_shift in range(WINDOW):
        for col_shift in range(WINDOW):
            tap_index = row_shift * WINDOW + col_shift
            moved_keys = jnp.roll(key_rows[row_shift:row_shift + NLAT], window_reach - col_shift, axis=1)
            moved_keys = moved_keys.astype(jnp.float32).reshape(NLAT, NLON, HEADS, HD)
            score_list.append(lax.optimization_barrier(jnp.sum(queries * moved_keys, axis=-1)) * score_scale + pos_bias[:, tap_index])
            moved_mask = jnp.roll(mask_rows[row_shift:row_shift + NLAT], window_reach - col_shift, axis=1)
            valid_list.append(jnp.logical_or(moved_mask > 0, tap_index == center))
    scores = jnp.stack(score_list)
    valid_mask = jnp.stack(valid_list)[..., None]
    row_top = lax.optimization_barrier(jnp.max(jnp.where(valid_mask, scores, -jnp.inf), axis=0, keepdims=True))
    raw_weights = jnp.exp(jnp.where(valid_mask, scores - row_top, -jnp.inf))
    weights = (raw_weights / lax.optimization_barrier(jnp.sum(raw_weights, axis=0, keepdims=True))).astype(jnp.bfloat16)
    attended = jnp.zeros((NLAT, NLON, HEADS, HD), jnp.float32)
    for row_shift in range(WINDOW):
        for col_shift in range(WINDOW):
            tap_index = row_shift * WINDOW + col_shift
            moved_values = jnp.roll(value_rows[row_shift:row_shift + NLAT], window_reach - col_shift, axis=1)
            moved_values = moved_values.astype(jnp.float32).reshape(NLAT, NLON, HEADS, HD)
            attended = attended + weights[tap_index][..., None].astype(jnp.float32) * moved_values
    attended = attended.reshape(cell_count, D).astype(jnp.bfloat16)
    residual = (state.reshape(cell_count, D).astype(jnp.float32) + jnp.dot(attended, out_weight, preferred_element_type=jnp.float32)).astype(jnp.bfloat16)
    second = layer_norm(residual, second_gain)
    land_flat = land_sea.reshape(cell_count, 1)
    tangent = cotangent.reshape(cell_count, D) * land_flat.astype(jnp.bfloat16)
    labels = regime.transpose(0, 2, 1, 3, 4).reshape(cell_count).astype(jnp.int32)
    sorted_ids = jnp.argsort(labels, stable=True).astype(jnp.int32)
    counts = lax.optimization_barrier(jnp.sum((labels[:, None] == jnp.arange(EXPERTS, dtype=jnp.int32)[None, :]).astype(jnp.int32), axis=0)).astype(jnp.int32)
    starts = (jnp.cumsum(counts) - counts).astype(jnp.int32)
    block_rows = 2048
    sorted_pad = jnp.concatenate([sorted_ids, jnp.full((block_rows,), cell_count, jnp.int32)])
    input_pad = jnp.concatenate([second, jnp.zeros((1, D), jnp.bfloat16)])
    tangent_pad = jnp.concatenate([tangent, jnp.zeros((1, D), jnp.bfloat16)])
    expert_out = jnp.zeros((cell_count + 1, D), jnp.bfloat16)
    up_list = []
    down_list = []
    for expert in range(EXPERTS):
        up_block = up_weight[:, expert * FF:(expert + 1) * FF]
        down_block = down_weight[expert * FF:(expert + 1) * FF]

        def block_step(block_index, state_carry):
            out_rows, acc_up, acc_down = state_carry
            offset = (starts[expert] + block_index * block_rows).astype(jnp.int32)
            picked = lax.dynamic_slice_in_dim(sorted_pad, offset, block_rows)
            inside = block_index * block_rows + jnp.arange(block_rows, dtype=jnp.int32) < counts[expert]
            picked = jnp.where(inside, picked, cell_count).astype(jnp.int32)
            row_data = input_pad[picked]
            row_tangent = tangent_pad[picked]
            hidden = jnp.dot(row_data, up_block, preferred_element_type=jnp.float32)
            active = gelu_value(hidden).astype(jnp.bfloat16)
            produced = jnp.dot(active, down_block, preferred_element_type=jnp.float32).astype(jnp.bfloat16)
            out_rows = out_rows.at[picked].set(produced)
            back_act = jnp.dot(row_tangent, down_block.T, preferred_element_type=jnp.float32)
            pre_act = (back_act * gelu_slope(hidden)).astype(jnp.bfloat16)
            acc_down = acc_down + jnp.dot(active.T, row_tangent, preferred_element_type=jnp.float32)
            acc_up = acc_up + jnp.dot(row_data.T, pre_act, preferred_element_type=jnp.float32)
            return (out_rows, acc_up, acc_down)
        block_total = ((counts[expert] + block_rows - 1) // block_rows).astype(jnp.int32)
        expert_out, acc_up, acc_down = lax.fori_loop(0, block_total, block_step, (expert_out, jnp.zeros((D, FF), jnp.float32), jnp.zeros((FF, D), jnp.float32)))
        up_list.append(acc_up)
        down_list.append(acc_down)
    grad_up = jnp.concatenate(up_list, axis=1)
    grad_down = jnp.concatenate(down_list, axis=0)
    block_out = (land_flat.astype(jnp.float32) * (residual.astype(jnp.float32) + expert_out[:cell_count].astype(jnp.float32))).astype(jnp.bfloat16)
    return (block_out.reshape(NLAT, NLON, D), grad_up, grad_down)
```

```python
import math

import jax
import jax.numpy as jnp
import numpy as np
from jax import lax
from jax.experimental import pallas as pl
from jax.experimental.pallas import tpu as pltpu
from jax.sharding import PartitionSpec as P

WINDOW = 7
REACH = WINDOW // 2
EXPERTS = 16
ROWS = 16
COLS = 8
CELLS = ROWS * COLS
D = 256
HEADS = 8
HD = 32
CAP = 16
SLOTS = EXPERTS * CAP
UNITS = 256
EXT = ROWS + 2 * REACH
LAND = 1024.0
FAR = -1e30
F32 = jnp.float32
BF = jnp.bfloat16
VMEM_LIMIT = 48 * 1024 * 1024


def vmem(count):
    return [pl.BlockSpec(memory_space=pltpu.VMEM)] * count


def dot(a, b):
    return lax.dot_general(a, b, (((1,), (0,)), ((), ())), preferred_element_type=F32)


def dot_t(a, b):
    return lax.dot_general(a, b, (((1,), (1,)), ((), ())), preferred_element_type=F32)


def t_dot(a, b):
    return lax.dot_general(a, b, (((0,), (0,)), ((), ())), preferred_element_type=F32)


def layer_norm(values, gain):
    mean_val = jnp.mean(values, axis=-1, keepdims=True)
    spread = jnp.mean(jnp.square(values - mean_val), axis=-1, keepdims=True)
    return ((values - mean_val) * lax.rsqrt(spread + 1e-05) * gain).astype(BF)


def tap_tables():
    column = np.concatenate([np.arange(8) + 3, np.arange(4) - 1, np.arange(4) + 11])
    table = np.zeros((WINDOW * WINDOW, 16, 8, 16), np.float32)
    for q in range(16):
        for a in range(8):
            for slot in range(16):
                da, db = a - q // 8, column[slot] - q % 8
                if 0 <= da < WINDOW and 0 <= db < WINDOW:
                    table[da * WINDOW + db, q, a, slot] = 1.0
    outside = (1.0 - table.sum(0)) * FAR
    return table.reshape(WINDOW * WINDOW, 2048), outside.reshape(1, 2048).astype(np.float32)


def prepare_kernel(pos_ref, taps_ref, outside_ref, labels_ref, cot_ref, land_ref, bias_ref, place_ref, sendc_ref):
    pos = pos_ref[...]
    high = pos.astype(BF)
    rest = pos - high.astype(F32)
    middle = rest.astype(BF)
    low = (rest - middle.astype(F32)).astype(BF)
    taps = taps_ref[...]
    bias = dot(high, taps) + dot(middle, taps) + dot(low, taps) + outside_ref[...]
    for q in range(16):
        bias_ref[q * 8 : q * 8 + 8, :] = bias[:, q * 128 : q * 128 + 128]
    labels = labels_ref[...]
    named = lax.broadcasted_iota(jnp.int32, (EXPERTS, CELLS), 0) == labels
    named = jnp.where(named, 1.0, 0.0)
    earlier = lax.broadcasted_iota(jnp.int32, (CELLS, CELLS), 0) < lax.broadcasted_iota(
        jnp.int32, (CELLS, CELLS), 1
    )
    before = dot(named.astype(BF), jnp.where(earlier, 1.0, 0.0).astype(BF))
    rank = jnp.sum(before * named, axis=0, keepdims=True)
    slot = labels * CAP + rank.astype(jnp.int32)
    place = lax.broadcasted_iota(jnp.int32, (SLOTS, CELLS), 0) == slot
    place = jnp.where(place, 1.0, 0.0).astype(BF)
    place_ref[...] = place
    tangent = cot_ref[...].astype(F32).reshape(CELLS, D) * land_ref[...].astype(F32)
    sendc_ref[...] = dot(place, tangent.astype(BF)).astype(BF)


def attention_kernel(
    own_ref,
    up_ref,
    down_ref,
    left_ref,
    right_ref,
    land_ref,
    gain1_ref,
    gain2_ref,
    project_ref,
    out_ref,
    bias_ref,
    place_ref,
    sendc_ref,
    residual_ref,
    send_ref,
    ext_ref,
    pen_ref,
):
    lat = lax.axis_index("lat")
    top = jnp.where(lat == 0, FAR, 0.0).astype(F32)
    bottom = jnp.where(lat == lax.axis_size("lat") - 1, FAR, 0.0).astype(F32)
    own3 = own_ref[...].astype(F32)
    up = up_ref[...].astype(F32)
    down = down_ref[...].astype(F32)
    left = left_ref[...].astype(F32)
    right = right_ref[...].astype(F32)

    def marked(piece):
        return jnp.where(piece[:, :, 0:128] > 0.5 * LAND, FAR, 0.0)

    ext_ref[0:REACH, 0:8, :] = up
    ext_ref[REACH : REACH + ROWS, 0:8, :] = own3
    ext_ref[REACH + ROWS : EXT, 0:8, :] = down
    ext_ref[:, 8:12, :] = left
    ext_ref[:, 12:16, :] = right
    land = land_ref[...].reshape(ROWS, COLS, 1)
    pen_ref[0:REACH, 0:8, :] = marked(up)
    pen_ref[REACH : REACH + ROWS, 0:8, :] = jnp.broadcast_to(
        jnp.where(land > 0, 0.0, FAR), (ROWS, COLS, 128)
    )
    pen_ref[REACH + ROWS : EXT, 0:8, :] = marked(down)
    pen_ref[:, 8:12, :] = marked(left)
    pen_ref[:, 12:16, :] = marked(right)
    pen_ref[0:REACH] = pen_ref[0:REACH] + top
    pen_ref[REACH + ROWS : EXT] = pen_ref[REACH + ROWS : EXT] + bottom
    own = own3.reshape(CELLS, D)
    gain1 = gain1_ref[...]
    normed = layer_norm(ext_ref[...].reshape(EXT * 16, D), gain1)
    keyvals = dot(normed, project_ref[:, D : 3 * D]).astype(BF)
    queries = dot(layer_norm(own, gain1), project_ref[:, 0:D]).astype(BF)
    pen = pen_ref[...].reshape(EXT * 16, 128).astype(BF)

    row = lax.broadcasted_iota(jnp.int32, (128, D), 0)
    lane = lax.broadcasted_iota(jnp.int32, (128, D), 1)
    head_mask = jnp.where(lane // HD == row % HEADS, 1.0, 0.0)
    spread = jnp.where(
        lax.broadcasted_iota(jnp.int32, (128, 16), 0) // HEADS
        == lax.broadcasted_iota(jnp.int32, (128, 16), 1),
        1.0,
        0.0,
    ).astype(BF)
    gather = jnp.where(
        lax.broadcasted_iota(jnp.int32, (16, 128), 1) // HEADS
        == lax.broadcasted_iota(jnp.int32, (16, 128), 0),
        1.0,
        0.0,
    ).astype(BF)
    row = lax.broadcasted_iota(jnp.int32, (128, 128), 0)
    lane = lax.broadcasted_iota(jnp.int32, (128, 128), 1)
    first_lane = jnp.where(lane == 0, 1.0, 0.0).astype(BF)
    query = row // HEADS
    centre = lane == (query // COLS + REACH) * 16 + query % COLS
    bias = bias_ref[...]
    scale = 1.0 / math.sqrt(HD)
    pieces = []
    for pair in range(ROWS // 2):
        keys = keyvals[32 * pair : 32 * pair + 128, 0:D]
        values = keyvals[32 * pair : 32 * pair + 128, D : 2 * D]
        wide = (dot(spread, queries[16 * pair : 16 * pair + 16]) * head_mask).astype(BF)
        closed = dot_t(first_lane, pen[32 * pair : 32 * pair + 128])
        scores = dot_t(wide, keys) * scale + bias + jnp.where(centre, 0.0, closed)
        raw = jnp.exp(scores - jnp.max(scores, axis=1, keepdims=True))
        weights = (raw / jnp.sum(raw, axis=1, keepdims=True)).astype(BF)
        taken = (dot(weights, values) * head_mask).astype(BF)
        pieces.append(dot(gather, taken))
    attended = jnp.concatenate(pieces, axis=0).astype(BF)
    residual = (own + dot(attended, out_ref[...])).astype(BF)
    residual_ref[...] = residual
    second = layer_norm(residual.astype(F32), gain2_ref[...])
    send_ref[:, 0:D] = dot(place_ref[...], second).astype(BF)
    send_ref[:, D : 2 * D] = sendc_ref[...]


def gelu_parts(hidden):
    half = 0.5 * (1.0 + lax.erf(hidden * 0.7071067811865476))
    slope = half + hidden * jnp.exp(-0.5 * hidden * hidden) * 0.3989422804014327
    return hidden * half, slope


def expert_kernel(got_ref, own_ref, *refs):
    weight_refs = (own_ref,) + refs[0:3]
    outputs_ref, keep_ref, give_ref, grad_ref = refs[3:]
    inputs = got_ref[:, 0:D]
    tangents = got_ref[:, D : 2 * D]
    outputs = jnp.zeros((SLOTS, D), F32)
    for member in range(4):
        up = weight_refs[member][0]
        down = weight_refs[member][1]
        active, slope = gelu_parts(dot(inputs, up))
        active = active.astype(BF)
        outputs = outputs + dot(active, down)
        pre_act = (dot_t(tangents, down) * slope).astype(BF)
        grad_ref[member, 0] = t_dot(inputs, pre_act)
        grad_ref[member, 1] = t_dot(active, tangents)
    outputs_ref[...] = outputs.astype(BF)
    lat = lax.axis_index("lat")
    for far in range(2):
        for other in range(2):
            start = pl.multiple_of(jnp.bitwise_xor(lat, 2 * far + other) * 64, 64)
            chunk = grad_ref[:, :, pl.ds(start, 64), :]
            if other:
                give_ref[far] = chunk.astype(BF)
            else:
                keep_ref[far] = chunk


def combine_kernel(returned_ref, place_ref, residual_ref, land_ref, block_ref):
    rows = lax.dot_general(
        place_ref[...],
        returned_ref[...],
        (((0,), (0,)), ((), ())),
        preferred_element_type=F32,
    )
    land = land_ref[...].astype(F32)
    block_ref[...] = (
        (land * (residual_ref[...].astype(F32) + rows)).astype(BF).reshape(ROWS, COLS, D)
    )


def gather_kernel(own_ref, a_ref, b_ref, c_ref, up_ref, down_ref):
    lat = lax.axis_index("lat")
    for mask, ref in enumerate((own_ref, a_ref, b_ref, c_ref)):
        start = pl.multiple_of(jnp.bitwise_xor(lat, mask) * 64, 64)
        up_ref[pl.ds(start, 64), :] = ref[0].astype(F32)
        down_ref[pl.ds(start, 64), :] = ref[1].astype(F32)


def call(kernel, outs, args, scratch=()):
    return pl.pallas_call(
        kernel,
        out_shape=[jax.ShapeDtypeStruct(shape, dtype) for shape, dtype in outs],
        in_specs=vmem(len(args)),
        out_specs=vmem(len(outs)),
        scratch_shapes=list(scratch),
        compiler_params=pltpu.CompilerParams(vmem_limit_bytes=VMEM_LIMIT),
    )(*args)


def shift(value, axis, step, closed):
    count = lax.axis_size(axis)
    pairs = [(i, (i + step) % count) for i in range(count) if closed or 0 <= i + step < count]
    return lax.ppermute(value, axis, pairs)


def swap(value, axis, mask):
    return lax.ppermute(value, axis, [(i, i ^ mask) for i in range(lax.axis_size(axis))])


def expert_groups():
    return [[8 * (e // 2) + (k if e % 2 == 0 else 7 - k) for e in range(EXPERTS)] for k in range(4)]


def exchange(value):
    return lax.all_to_all(
        value, "lon", 0, 0, axis_index_groups=expert_groups(), tiled=True
    )


def on_device(
    state,
    cotangent,
    land_sea,
    regime,
    first_gain,
    second_gain,
    project_weight,
    out_weight,
    pos_bias,
    up_weight,
    down_weight,
):
    marked = jnp.where(land_sea[:, :, None] > 0, state, jnp.asarray(LAND, BF))
    up = shift(marked[ROWS - REACH :], "lat", 1, False)
    down = shift(marked[:REACH], "lat", -1, False)
    tall = jnp.concatenate([up, marked, down], axis=0)
    left = shift(tall[:, COLS - 4 :], "lon", 1, True)
    right = shift(tall[:, :4], "lon", -1, True)

    land_column = land_sea.reshape(CELLS, 1)
    taps, outside = tap_tables()
    bias, place, sendc = call(
        prepare_kernel,
        [((128, 128), F32), ((SLOTS, CELLS), BF), ((SLOTS, D), BF)],
        (
            pos_bias,
            jnp.asarray(taps, BF),
            jnp.asarray(outside),
            regime.reshape(1, CELLS),
            cotangent,
            land_column,
        ),
    )
    weights = [jnp.stack([up_weight, down_weight])]
    for mask in (1, 2, 3):
        weights.append(swap(weights[0], "lon", mask))

    residual, send = call(
        attention_kernel,
        [((CELLS, D), BF), ((SLOTS, 2 * D), BF)],
        (
            state,
            up,
            down,
            left,
            right,
            land_column,
            first_gain.reshape(1, D),
            second_gain.reshape(1, D),
            project_weight,
            out_weight,
            bias,
            place,
            sendc,
        ),
        (pltpu.VMEM((EXT, 16, D), F32), pltpu.VMEM((EXT, 16, 128), F32)),
    )
    got = exchange(send.reshape(EXPERTS, CAP, 2 * D)).reshape(SLOTS, 2 * D)
    outputs, keep, give = call(
        expert_kernel,
        [((SLOTS, D), BF), ((2, 4, 2, 64, D), F32), ((2, 4, 2, 64, D), BF)],
        (got, *weights),
        (pltpu.VMEM((4, 2, 256, D), F32),),
    )
    returned = exchange(outputs.reshape(EXPERTS, CAP, D)).reshape(SLOTS, D)

    near = swap(give, "lat", 1)
    far = swap((keep[1] + near[1].astype(F32)).astype(BF), "lat", 2)
    part = keep[0] + near[0].astype(F32) + far.astype(F32)
    total = part[0]
    for mask in (1, 2, 3):
        total = total + swap(part[mask].astype(BF), "lon", mask).astype(F32)
    total = total.astype(BF)
    grad_up, grad_down = call(
        gather_kernel,
        [((D, UNITS), F32), ((UNITS, D), F32)],
        (total, *[swap(total, "lat", mask) for mask in (1, 2, 3)]),
    )
    (block,) = call(
        combine_kernel,
        [((ROWS, COLS, D), BF)],
        (returned, place, residual, land_column),
    )
    return block, grad_up, grad_down


def solution(mesh):
    placed = (
        P("lat", "lon", None),
        P("lat", "lon", None),
        P("lat", "lon"),
        P("lat", "lon", None, None, None),
        P(),
        P(),
        P(),
        P(),
        P(),
        P(None, "lon"),
        P("lon", None),
    )
    return jax.shard_map(
        on_device,
        mesh=mesh,
        in_specs=placed,
        out_specs=(P("lat", "lon", None), P(None, "lon"), P("lon", None)),
        check_vma=False,
    )
```

```python
import math

import jax
import jax.numpy as jnp
import numpy as np
from jax import lax
from jax.experimental import pallas as pl
from jax.experimental.pallas import tpu as pltpu
from jax.sharding import PartitionSpec as P

WINDOW = 7
REACH = WINDOW // 2
EXPERTS = 16
ROWS = 16
COLS = 8
CELLS = ROWS * COLS
D = 256
HEADS = 8
HD = 32
CAP = 16
SLOTS = EXPERTS * CAP
UNITS = 256
EXT = ROWS + 2 * REACH
LAND = 1024.0
FAR = -1e30
F32 = jnp.float32
BF = jnp.bfloat16
VMEM_LIMIT = 48 * 1024 * 1024


def vmem(count):
    return [pl.BlockSpec(memory_space=pltpu.VMEM)] * count


def dot(a, b):
    return lax.dot_general(a, b, (((1,), (0,)), ((), ())), preferred_element_type=F32)


def dot_t(a, b):
    return lax.dot_general(a, b, (((1,), (1,)), ((), ())), preferred_element_type=F32)


def t_dot(a, b):
    return lax.dot_general(a, b, (((0,), (0,)), ((), ())), preferred_element_type=F32)


def layer_norm(values, gain):
    mean_val = jnp.mean(values, axis=-1, keepdims=True)
    spread = jnp.mean(jnp.square(values - mean_val), axis=-1, keepdims=True)
    return ((values - mean_val) * lax.rsqrt(spread + 1e-05) * gain).astype(BF)


def tap_tables():
    column = np.concatenate([np.arange(8) + 3, np.arange(4) - 1, np.arange(4) + 11])
    table = np.zeros((WINDOW * WINDOW, 16, 8, 16), np.float32)
    for q in range(16):
        for a in range(8):
            for slot in range(16):
                da, db = a - q // 8, column[slot] - q % 8
                if 0 <= da < WINDOW and 0 <= db < WINDOW:
                    table[da * WINDOW + db, q, a, slot] = 1.0
    outside = (1.0 - table.sum(0)) * FAR
    return table.reshape(WINDOW * WINDOW, 2048), outside.reshape(1, 2048).astype(np.float32)


def mark_kernel(state_ref, land_ref, marked_ref, even_ref, odd_ref):
    land = jnp.broadcast_to(land_ref[...][:, :, None], (ROWS, COLS, D))
    marked = jnp.where(land > 0, state_ref[...].astype(F32), LAND).astype(BF)
    marked_ref[...] = marked
    even = lax.axis_index("lat") & 1 == 0
    top, bottom = marked[:REACH], marked[ROWS - REACH :]
    even_ref[...] = jnp.where(even, bottom, top)
    odd_ref[...] = jnp.where(even, top, bottom)


def prepare_kernel(pos_ref, taps_ref, outside_ref, labels_ref, cot_ref, land_ref, bias_ref, place_ref, sendc_ref):
    pos = pos_ref[...]
    high = pos.astype(BF)
    rest = pos - high.astype(F32)
    middle = rest.astype(BF)
    low = (rest - middle.astype(F32)).astype(BF)
    taps = taps_ref[...]
    bias = dot(high, taps) + dot(middle, taps) + dot(low, taps) + outside_ref[...]
    for q in range(16):
        bias_ref[q * 8 : q * 8 + 8, :] = bias[:, q * 128 : q * 128 + 128]
    labels = labels_ref[...]
    named = lax.broadcasted_iota(jnp.int32, (EXPERTS, CELLS), 0) == labels
    named = jnp.where(named, 1.0, 0.0)
    earlier = lax.broadcasted_iota(jnp.int32, (CELLS, CELLS), 0) < lax.broadcasted_iota(
        jnp.int32, (CELLS, CELLS), 1
    )
    before = dot(named.astype(BF), jnp.where(earlier, 1.0, 0.0).astype(BF))
    rank = jnp.sum(before * named, axis=0, keepdims=True)
    slot = labels * CAP + rank.astype(jnp.int32)
    place = lax.broadcasted_iota(jnp.int32, (SLOTS, CELLS), 0) == slot
    place = jnp.where(place, 1.0, 0.0).astype(BF)
    place_ref[...] = place
    tangent = cot_ref[...].astype(F32).reshape(CELLS, D) * land_ref[...].astype(F32)
    sendc_ref[...] = dot(place, tangent.astype(BF)).astype(BF)


def in_order(axis, even_ref, odd_ref):
    even, odd = even_ref[...].astype(F32), odd_ref[...].astype(F32)
    at_even = lax.axis_index(axis) & 1 == 0
    return jnp.where(at_even, odd, even), jnp.where(at_even, even, odd)


def attention_kernel(
    own_ref,
    lat_even_ref,
    lat_odd_ref,
    lon_even_ref,
    lon_odd_ref,
    land_ref,
    gain1_ref,
    gain2_ref,
    project_ref,
    out_ref,
    bias_ref,
    place_ref,
    sendc_ref,
    near_ref,
    middle_ref,
    far_ref,
    residual_ref,
    send_ref,
    fetched_ref,
    ext_ref,
    pen_ref,
):
    fetched_ref[0] = near_ref[...]
    fetched_ref[1] = middle_ref[...]
    fetched_ref[2] = far_ref[...]
    lat = lax.axis_index("lat")
    top = jnp.where(lat == 0, FAR, 0.0).astype(F32)
    bottom = jnp.where(lat == lax.axis_size("lat") - 1, FAR, 0.0).astype(F32)
    own3 = own_ref[...].astype(F32)
    up, down = in_order("lat", lat_even_ref, lat_odd_ref)
    left, right = in_order("lon", lon_even_ref, lon_odd_ref)

    def marked(piece):
        return jnp.where(piece[:, :, 0:128] > 0.5 * LAND, FAR, 0.0)

    ext_ref[0:REACH, 0:8, :] = up
    ext_ref[REACH : REACH + ROWS, 0:8, :] = own3
    ext_ref[REACH + ROWS : EXT, 0:8, :] = down
    ext_ref[:, 8:12, :] = left
    ext_ref[:, 12:16, :] = right
    land = land_ref[...].reshape(ROWS, COLS, 1)
    pen_ref[0:REACH, 0:8, :] = marked(up)
    pen_ref[REACH : REACH + ROWS, 0:8, :] = jnp.broadcast_to(
        jnp.where(land > 0, 0.0, FAR), (ROWS, COLS, 128)
    )
    pen_ref[REACH + ROWS : EXT, 0:8, :] = marked(down)
    pen_ref[:, 8:12, :] = marked(left)
    pen_ref[:, 12:16, :] = marked(right)
    pen_ref[0:REACH] = pen_ref[0:REACH] + top
    pen_ref[REACH + ROWS : EXT] = pen_ref[REACH + ROWS : EXT] + bottom
    own = own3.reshape(CELLS, D)
    gain1 = gain1_ref[...]
    normed = layer_norm(ext_ref[...].reshape(EXT * 16, D), gain1)
    keyvals = dot(normed, project_ref[:, D : 3 * D]).astype(BF)
    queries = dot(layer_norm(own, gain1), project_ref[:, 0:D]).astype(BF)
    pen = pen_ref[...].reshape(EXT * 16, 128).astype(BF)

    row = lax.broadcasted_iota(jnp.int32, (128, D), 0)
    lane = lax.broadcasted_iota(jnp.int32, (128, D), 1)
    head_mask = jnp.where(lane // HD == row % HEADS, 1.0, 0.0)
    spread = jnp.where(
        lax.broadcasted_iota(jnp.int32, (128, 16), 0) // HEADS
        == lax.broadcasted_iota(jnp.int32, (128, 16), 1),
        1.0,
        0.0,
    ).astype(BF)
    gather = jnp.where(
        lax.broadcasted_iota(jnp.int32, (16, 128), 1) // HEADS
        == lax.broadcasted_iota(jnp.int32, (16, 128), 0),
        1.0,
        0.0,
    ).astype(BF)
    row = lax.broadcasted_iota(jnp.int32, (128, 128), 0)
    lane = lax.broadcasted_iota(jnp.int32, (128, 128), 1)
    first_lane = jnp.where(lane == 0, 1.0, 0.0).astype(BF)
    query = row // HEADS
    centre = lane == (query // COLS + REACH) * 16 + query % COLS
    bias = bias_ref[...]
    scale = 1.0 / math.sqrt(HD)
    pieces = []
    for pair in range(ROWS // 2):
        keys = keyvals[32 * pair : 32 * pair + 128, 0:D]
        values = keyvals[32 * pair : 32 * pair + 128, D : 2 * D]
        wide = (dot(spread, queries[16 * pair : 16 * pair + 16]) * head_mask).astype(BF)
        closed = dot_t(first_lane, pen[32 * pair : 32 * pair + 128])
        scores = dot_t(wide, keys) * scale + bias + jnp.where(centre, 0.0, closed)
        raw = jnp.exp(scores - jnp.max(scores, axis=1, keepdims=True))
        weights = (raw / jnp.sum(raw, axis=1, keepdims=True)).astype(BF)
        taken = (dot(weights, values) * head_mask).astype(BF)
        pieces.append(dot(gather, taken))
    attended = jnp.concatenate(pieces, axis=0).astype(BF)
    residual = (own + dot(attended, out_ref[...])).astype(BF)
    residual_ref[...] = residual
    second = layer_norm(residual.astype(F32), gain2_ref[...])
    send_ref[:, 0:D] = dot(place_ref[...], second).astype(BF)
    send_ref[:, D : 2 * D] = sendc_ref[...]


def gelu_parts(hidden):
    half = 0.5 * (1.0 + lax.erf(hidden * 0.7071067811865476))
    slope = half + hidden * jnp.exp(-0.5 * hidden * hidden) * 0.3989422804014327
    return hidden * half, slope


def expert_kernel(
    got_ref, up_ref, down_ref, mine_ref, other_ref, outputs_ref, keep_ref, give_ref, grad_ref
):
    lat = lax.axis_index("lat")
    first_core = lat & 1 == 0
    inputs = got_ref[:, 0:D]
    tangents = got_ref[:, D : 2 * D]
    outputs = jnp.zeros((SLOTS, D), F32)
    for member in range(4):
        if member:
            mine = mine_ref[member - 1]
            other = other_ref[member - 1]
            up = jnp.where(first_core, mine, other)
            down = jnp.where(first_core, other, mine)
        else:
            up = up_ref[...]
            down = down_ref[...]
        active, slope = gelu_parts(dot(inputs, up))
        active = active.astype(BF)
        outputs = outputs + dot(active, down)
        pre_act = (dot_t(tangents, down) * slope).astype(BF)
        grad_ref[member, 0] = t_dot(inputs, pre_act)
        grad_ref[member, 1] = t_dot(active, tangents)
    outputs_ref[...] = outputs.astype(BF)
    for far in range(2):
        for other in range(2):
            start = pl.multiple_of(jnp.bitwise_xor(lat, 2 * far + other) * 64, 64)
            chunk = grad_ref[:, :, pl.ds(start, 64), :]
            if other:
                give_ref[far] = chunk.astype(BF)
            else:
                keep_ref[far] = chunk


def combine_kernel(
    returned_ref, place_ref, residual_ref, land_ref, part_ref, a_ref, b_ref, c_ref, block_ref, total_ref
):
    rows = t_dot(place_ref[...], returned_ref[...])
    land = land_ref[...].astype(F32)
    block_ref[...] = (
        (land * (residual_ref[...].astype(F32) + rows)).astype(BF).reshape(ROWS, COLS, D)
    )
    total = part_ref[...] + a_ref[...].astype(F32)
    total_ref[...] = (total + b_ref[...].astype(F32) + c_ref[...].astype(F32)).astype(BF)


def gather_kernel(own_ref, a_ref, b_ref, c_ref, up_ref, down_ref):
    lat = lax.axis_index("lat")
    for mask, ref in enumerate((own_ref, a_ref, b_ref, c_ref)):
        start = pl.multiple_of(jnp.bitwise_xor(lat, mask) * 64, 64)
        up_ref[pl.ds(start, 64), :] = ref[0].astype(F32)
        down_ref[pl.ds(start, 64), :] = ref[1].astype(F32)


def call(kernel, outs, args, scratch=()):
    return pl.pallas_call(
        kernel,
        out_shape=[jax.ShapeDtypeStruct(shape, dtype) for shape, dtype in outs],
        in_specs=vmem(len(args)),
        out_specs=vmem(len(outs)),
        scratch_shapes=list(scratch),
        compiler_params=pltpu.CompilerParams(vmem_limit_bytes=VMEM_LIMIT),
    )(*args)


def pair_up(value, axis, first, closed):
    count = lax.axis_size(axis)
    pairs = []
    for i in range(first, count if closed else count - 1, 2):
        pairs += [(i, (i + 1) % count), ((i + 1) % count, i)]
    return lax.ppermute(value, axis, pairs)


def swap(value, axis, mask):
    return lax.ppermute(value, axis, [(i, i ^ mask) for i in range(lax.axis_size(axis))])


def expert_groups():
    groups = []
    for lat in range(4):
        for k in range(4):
            group = []
            for e in range(EXPERTS):
                place = lat ^ 2 if (e // 2) % 2 else lat
                group.append(place * 64 + 8 * (e // 2) + (7 - k if e % 2 else k))
            groups.append(group)
    return groups


def exchange(value):
    return lax.all_to_all(
        value, ("lat", "lon"), 0, 0, axis_index_groups=expert_groups(), tiled=True
    )


def on_device(
    state,
    cotangent,
    land_sea,
    regime,
    first_gain,
    second_gain,
    project_weight,
    out_weight,
    pos_bias,
    up_weight,
    down_weight,
):
    marked, even, odd = call(
        mark_kernel,
        [((ROWS, COLS, D), BF), ((REACH, COLS, D), BF), ((REACH, COLS, D), BF)],
        (state, land_sea),
    )
    lat_even = pair_up(even, "lat", 0, False)
    lat_odd = pair_up(odd, "lat", 1, False)
    at_even = lax.axis_index("lat") & 1 == 0
    up = jnp.where(at_even, lat_odd, lat_even)
    down = jnp.where(at_even, lat_even, lat_odd)
    tall = jnp.concatenate([up, marked, down], axis=0)
    at_even = lax.axis_index("lon") & 1 == 0
    lon_odd = pair_up(jnp.where(at_even, tall[:, :4], tall[:, 4:]), "lon", 1, True)
    lon_even = pair_up(jnp.where(at_even, tall[:, 4:], tall[:, :4]), "lon", 0, True)

    land_column = land_sea.reshape(CELLS, 1)
    taps, outside = tap_tables()
    bias, place, sendc = call(
        prepare_kernel,
        [((128, 128), F32), ((SLOTS, CELLS), BF), ((SLOTS, D), BF)],
        (
            pos_bias,
            jnp.asarray(taps, BF),
            jnp.asarray(outside),
            regime.reshape(1, CELLS),
            cotangent,
            land_column,
        ),
    )
    half = jnp.where(lax.axis_index("lat") & 1 == 0, up_weight, down_weight)
    fetched = [swap(half, "lon", mask) for mask in (1, 2, 3)]

    residual, send, fetched = call(
        attention_kernel,
        [((CELLS, D), BF), ((SLOTS, 2 * D), BF), ((3, D, UNITS), BF)],
        (
            state,
            lat_even,
            lat_odd,
            lon_even,
            lon_odd,
            land_column,
            first_gain.reshape(1, D),
            second_gain.reshape(1, D),
            project_weight,
            out_weight,
            bias,
            place,
            sendc,
            *fetched,
        ),
        (pltpu.VMEM((EXT, 16, D), F32), pltpu.VMEM((EXT, 16, 128), F32)),
    )
    got = exchange(send.reshape(EXPERTS, CAP, 2 * D)).reshape(SLOTS, 2 * D)
    outputs, keep, give = call(
        expert_kernel,
        [((SLOTS, D), BF), ((2, 4, 2, 64, D), F32), ((2, 4, 2, 64, D), BF)],
        (got, up_weight, down_weight, fetched, swap(fetched, "lat", 1)),
        (pltpu.VMEM((4, 2, 256, D), F32),),
    )
    near = swap(give, "lat", 1)
    sent = (keep[1] + near[1].astype(F32)).astype(BF)
    outputs, sent = lax.optimization_barrier((outputs, sent))
    returned = exchange(outputs.reshape(EXPERTS, CAP, D)).reshape(SLOTS, D)
    far = swap(sent, "lat", 2)
    part = keep[0] + near[0].astype(F32) + far.astype(F32)
    others = [swap(part[mask].astype(BF), "lon", mask) for mask in (1, 2, 3)]
    block, total = call(
        combine_kernel,
        [((ROWS, COLS, D), BF), ((2, 64, D), BF)],
        (returned, place, residual, land_column, part[0], *others),
    )
    grad_up, grad_down = call(
        gather_kernel,
        [((D, UNITS), F32), ((UNITS, D), F32)],
        (total, *[swap(total, "lat", mask) for mask in (1, 2, 3)]),
    )
    return block, grad_up, grad_down


def solution(mesh):
    placed = (
        P("lat", "lon", None),
        P("lat", "lon", None),
        P("lat", "lon"),
        P("lat", "lon", None, None, None),
        P(),
        P(),
        P(),
        P(),
        P(),
        P(None, "lon"),
        P("lon", None),
    )
    return jax.shard_map(
        on_device,
        mesh=mesh,
        in_specs=placed,
        out_specs=(P("lat", "lon", None), P(None, "lon"), P("lon", None)),
        check_vma=False,
    )
```

```python
import math

import jax
import jax.numpy as jnp
import numpy as np
from jax import lax
from jax.experimental import pallas as pl
from jax.experimental.pallas import tpu as pltpu
from jax.sharding import PartitionSpec as P

WINDOW = 7
REACH = WINDOW // 2
EXPERTS = 16
ROWS = 16
COLS = 8
CELLS = ROWS * COLS
D = 256
HEADS = 8
HD = 32
CAP = 16
SLOTS = EXPERTS * CAP
UNITS = 256
EXT = ROWS + 2 * REACH
LAND = 1024.0
FAR = -1e30
F32 = jnp.float32
BF = jnp.bfloat16
VMEM_LIMIT = 48 * 1024 * 1024


def vmem(count):
    return [pl.BlockSpec(memory_space=pltpu.VMEM)] * count


def dot(a, b):
    return lax.dot_general(a, b, (((1,), (0,)), ((), ())), preferred_element_type=F32)


def dot_t(a, b):
    return lax.dot_general(a, b, (((1,), (1,)), ((), ())), preferred_element_type=F32)


def t_dot(a, b):
    return lax.dot_general(a, b, (((0,), (0,)), ((), ())), preferred_element_type=F32)


def layer_norm(values, gain):
    mean_val = jnp.mean(values, axis=-1, keepdims=True)
    spread = jnp.mean(jnp.square(values - mean_val), axis=-1, keepdims=True)
    return ((values - mean_val) * lax.rsqrt(spread + 1e-05) * gain).astype(BF)


def tap_tables():
    column = np.concatenate([np.arange(8) + 3, np.arange(4) - 1, np.arange(4) + 11])
    table = np.zeros((WINDOW * WINDOW, 16, 8, 16), np.float32)
    for q in range(16):
        for a in range(8):
            for slot in range(16):
                da, db = a - q // 8, column[slot] - q % 8
                if 0 <= da < WINDOW and 0 <= db < WINDOW:
                    table[da * WINDOW + db, q, a, slot] = 1.0
    outside = (1.0 - table.sum(0)) * FAR
    return table.reshape(WINDOW * WINDOW, 2048), outside.reshape(1, 2048).astype(np.float32)


def column(table):
    return jnp.concatenate([table[:, i : i + 1] for i in range(ROWS)], axis=0)


def mark_kernel(state_ref, land_ref, up_ref, down_ref, marked_ref, even_ref, odd_ref, half_ref):
    even = lax.axis_index("lat") & 1 == 0
    land = column(land_ref[...]).reshape(ROWS, COLS, 1)
    marked = jnp.where(land > 0, state_ref[...].astype(F32), LAND).astype(BF)
    marked_ref[...] = marked
    top, bottom = marked[:REACH], marked[ROWS - REACH :]
    even_ref[...] = jnp.where(even, bottom, top)
    odd_ref[...] = jnp.where(even, top, bottom)
    half_ref[...] = jnp.where(even, up_ref[...], down_ref[...])


def prepare_kernel(
    pos_ref,
    taps_ref,
    outside_ref,
    labels_ref,
    cot_ref,
    land_ref,
    state_ref,
    gain1_ref,
    gain2_ref,
    project_ref,
    bias_ref,
    place_ref,
    sendc_ref,
    triple_ref,
    gains_ref,
):
    land = column(land_ref[...])
    gains_ref[0:1] = gain1_ref[...]
    gains_ref[1:2] = gain2_ref[...]
    own = state_ref[...].astype(F32).reshape(CELLS, D)
    triple_ref[...] = dot(layer_norm(own, gain1_ref[...]), project_ref[...]).astype(BF)
    pos = pos_ref[...]
    high = pos.astype(BF)
    rest = pos - high.astype(F32)
    middle = rest.astype(BF)
    low = (rest - middle.astype(F32)).astype(BF)
    taps = taps_ref[...]
    bias = dot(high, taps) + dot(middle, taps) + dot(low, taps) + outside_ref[...]
    for q in range(16):
        bias_ref[q * 8 : q * 8 + 8, :] = bias[:, q * 128 : q * 128 + 128]
    labels = column(labels_ref[...])
    named = lax.broadcasted_iota(jnp.int32, (CELLS, EXPERTS), 1) == labels
    named = jnp.where(named, 1.0, 0.0)
    earlier = lax.broadcasted_iota(jnp.int32, (CELLS, CELLS), 1) < lax.broadcasted_iota(
        jnp.int32, (CELLS, CELLS), 0
    )
    before = dot(jnp.where(earlier, 1.0, 0.0).astype(BF), named.astype(BF))
    rank = jnp.sum(before * named, axis=1, keepdims=True)
    slot = labels * CAP + rank.astype(jnp.int32)
    place = lax.broadcasted_iota(jnp.int32, (CELLS, SLOTS), 1) == slot
    place = jnp.where(place, 1.0, 0.0).astype(BF)
    place_ref[...] = place
    tangent = cot_ref[...].astype(F32).reshape(CELLS, D) * land.astype(F32)
    sendc_ref[...] = t_dot(place, tangent.astype(BF)).astype(BF)


def in_order(axis, even_ref, odd_ref):
    even, odd = even_ref[...].astype(F32), odd_ref[...].astype(F32)
    at_even = lax.axis_index(axis) & 1 == 0
    return jnp.where(at_even, odd, even), jnp.where(at_even, even, odd)


def attention_kernel(
    own_ref,
    lat_even_ref,
    lat_odd_ref,
    lon_even_ref,
    lon_odd_ref,
    land_ref,
    gains_ref,
    triple_ref,
    project_ref,
    out_ref,
    bias_ref,
    place_ref,
    sendc_ref,
    half_ref,
    near_ref,
    residual_ref,
    send_ref,
    fetched_ref,
    side_ref,
    pen_ref,
):
    fetched_ref[0] = half_ref[...]
    fetched_ref[1] = near_ref[...]
    lat = lax.axis_index("lat")
    top = jnp.where(lat == 0, FAR, 0.0).astype(F32)
    bottom = jnp.where(lat == lax.axis_size("lat") - 1, FAR, 0.0).astype(F32)
    up, down = in_order("lat", lat_even_ref, lat_odd_ref)
    left, right = in_order("lon", lon_even_ref, lon_odd_ref)
    side_ref[:, 0:4] = left
    side_ref[:, 4:8] = right
    side = side_ref[...]

    def marked(piece):
        return jnp.where(piece[:, :, 0:128] > 0.5 * LAND, FAR, 0.0)

    own_rows = pl.ds(REACH, ROWS)
    land = column(land_ref[...]).reshape(ROWS, COLS, 1)
    pen_ref[:, 8:16] = marked(side)
    pen_ref[0:REACH, 0:8] = marked(up)
    pen_ref[own_rows, 0:8] = jnp.broadcast_to(jnp.where(land > 0, 0.0, FAR), (ROWS, COLS, 128))
    pen_ref[REACH + ROWS : EXT, 0:8] = marked(down)
    pen_ref[0:REACH] = pen_ref[0:REACH] + top
    pen_ref[REACH + ROWS : EXT] = pen_ref[REACH + ROWS : EXT] + bottom
    pen = pen_ref[...].reshape(EXT * 16, 128).astype(BF)

    halo = jnp.concatenate([side, up, down], axis=0).reshape((EXT + 2 * REACH) * 8, D)
    halo = dot(layer_norm(halo, gains_ref[0:1]), project_ref[:, D : 3 * D])
    halo = halo.reshape(EXT + 2 * REACH, 8, 2 * D)
    middle = triple_ref[:, D : 3 * D].astype(F32).reshape(ROWS, COLS, 2 * D)
    middle = jnp.concatenate([halo[EXT : EXT + REACH], middle, halo[EXT + REACH :]], axis=0)
    keyvals = jnp.concatenate([middle, halo[:EXT]], axis=1).reshape(EXT * 16, 2 * D).astype(BF)
    queries = triple_ref[:, 0:D]
    own = own_ref[...].astype(F32).reshape(CELLS, D)

    row = lax.broadcasted_iota(jnp.int32, (128, D), 0)
    lane = lax.broadcasted_iota(jnp.int32, (128, D), 1)
    head_mask = jnp.where(lane // HD == row % HEADS, 1.0, 0.0)
    spread = jnp.where(
        lax.broadcasted_iota(jnp.int32, (128, 16), 0) // HEADS
        == lax.broadcasted_iota(jnp.int32, (128, 16), 1),
        1.0,
        0.0,
    ).astype(BF)
    gather = jnp.where(
        lax.broadcasted_iota(jnp.int32, (16, 128), 1) // HEADS
        == lax.broadcasted_iota(jnp.int32, (16, 128), 0),
        1.0,
        0.0,
    ).astype(BF)
    row = lax.broadcasted_iota(jnp.int32, (128, 128), 0)
    lane = lax.broadcasted_iota(jnp.int32, (128, 128), 1)
    first_lane = jnp.where(lane[0:8] == 0, 1.0, 0.0).astype(BF)
    query = row // HEADS
    centre = lane == (query // COLS + REACH) * 16 + query % COLS
    bias = bias_ref[...]
    scale = 1.0 / math.sqrt(HD)
    closed = dot_t(first_lane, pen)
    pairs = range(ROWS // 2)
    scores = []
    for pair in pairs:
        wide = (dot(spread, queries[16 * pair : 16 * pair + 16]) * head_mask).astype(BF)
        scores.append(dot_t(wide, keyvals[32 * pair : 32 * pair + 128, 0:D]))
    weights = []
    for pair in pairs:
        shut = jnp.concatenate([closed[:, 32 * pair : 32 * pair + 128]] * 16, axis=0)
        score = scores[pair] * scale + bias + jnp.where(centre, 0.0, shut)
        raw = jnp.exp(score - jnp.max(score, axis=1, keepdims=True))
        weights.append((raw / jnp.sum(raw, axis=1, keepdims=True)).astype(BF))
    pieces = []
    for pair in pairs:
        taken = dot(weights[pair], keyvals[32 * pair : 32 * pair + 128, D : 2 * D])
        pieces.append(dot(gather, (taken * head_mask).astype(BF)))
    attended = jnp.concatenate(pieces, axis=0).astype(BF)
    residual = (own + dot(attended, out_ref[...])).astype(BF)
    residual_ref[...] = residual
    second = layer_norm(residual.astype(F32), gains_ref[1:2])
    send_ref[:, 0:D] = t_dot(place_ref[...], second).astype(BF)
    send_ref[:, D : 2 * D] = sendc_ref[...]


def gelu_parts(hidden):
    half = 0.5 * (1.0 + lax.erf(hidden * 0.7071067811865476))
    slope = half + hidden * jnp.exp(-0.5 * hidden * hidden) * 0.3989422804014327
    return hidden * half, slope


def expert_kernel(
    got_ref,
    up_ref,
    down_ref,
    mine1_ref,
    mine2_ref,
    other1_ref,
    other2_ref,
    outputs_ref,
    keep_ref,
    give_ref,
    grad_ref,
):
    lat = lax.axis_index("lat")
    first_core = lat & 1 == 0
    inputs = got_ref[:, 0:D]
    tangents = got_ref[:, D : 2 * D]
    outputs = jnp.zeros((SLOTS, D), F32)
    for member in range(4):
        if member:
            mine = mine1_ref[...] if member == 1 else mine2_ref[member - 2]
            other = other1_ref[...] if member == 1 else other2_ref[member - 2]
            up = jnp.where(first_core, mine, other)
            down = jnp.where(first_core, other, mine)
        else:
            up = up_ref[...]
            down = down_ref[...]
        active, slope = gelu_parts(dot(inputs, up))
        active = active.astype(BF)
        outputs = outputs + dot(active, down)
        pre_act = (dot_t(tangents, down) * slope).astype(BF)
        grad_ref[member, 0] = t_dot(inputs, pre_act)
        grad_ref[member, 1] = t_dot(active, tangents)
    outputs_ref[...] = outputs.astype(BF)
    for far in range(2):
        for other in range(2):
            start = pl.multiple_of(jnp.bitwise_xor(lat, 2 * far + other) * 64, 64)
            chunk = grad_ref[:, :, pl.ds(start, 64), :]
            if other:
                give_ref[far] = chunk.astype(BF)
            else:
                keep_ref[far] = chunk


def combine_kernel(
    returned_ref, place_ref, residual_ref, land_ref, part_ref, a_ref, b_ref, c_ref, block_ref, total_ref
):
    rows = dot(place_ref[...], returned_ref[...])
    land = column(land_ref[...]).astype(F32)
    block_ref[...] = (
        (land * (residual_ref[...].astype(F32) + rows)).astype(BF).reshape(ROWS, COLS, D)
    )
    total = part_ref[...] + a_ref[...].astype(F32)
    total_ref[...] = (total + b_ref[...].astype(F32) + c_ref[...].astype(F32)).astype(BF)


def gather_kernel(own_ref, a_ref, b_ref, c_ref, up_ref, down_ref):
    lat = lax.axis_index("lat")
    for mask, ref in enumerate((own_ref, a_ref, b_ref, c_ref)):
        start = pl.multiple_of(jnp.bitwise_xor(lat, mask) * 64, 64)
        up_ref[pl.ds(start, 64), :] = ref[0].astype(F32)
        down_ref[pl.ds(start, 64), :] = ref[1].astype(F32)


def call(kernel, outs, args, scratch=(), fetch=0):
    def fetching(*refs):
        kept = len(args) + len(outs) + len(scratch)
        copies = [
            pltpu.make_async_copy(refs[i], refs[kept + i], refs[-1].at[i]) for i in range(fetch)
        ]
        for copy in copies:
            copy.start()
        for copy in copies:
            copy.wait()
        kernel(*refs[kept : kept + fetch], *refs[fetch:kept])

    spaces = [pltpu.HBM] * fetch + [pltpu.VMEM] * (len(args) - fetch)
    landing = [pltpu.VMEM(arg.shape, arg.dtype) for arg in args[:fetch]]
    if fetch:
        landing.append(pltpu.SemaphoreType.DMA((fetch,)))
    return pl.pallas_call(
        fetching if fetch else kernel,
        out_shape=[jax.ShapeDtypeStruct(shape, dtype) for shape, dtype in outs],
        in_specs=[pl.BlockSpec(memory_space=space) for space in spaces],
        out_specs=vmem(len(outs)),
        scratch_shapes=list(scratch) + landing,
        compiler_params=pltpu.CompilerParams(vmem_limit_bytes=None if fetch else VMEM_LIMIT),
    )(*args)


def pair_up(value, axis, first, closed):
    count = lax.axis_size(axis)
    pairs = []
    for i in range(first, count if closed else count - 1, 2):
        pairs += [(i, (i + 1) % count), ((i + 1) % count, i)]
    return lax.ppermute(value, axis, pairs)


def swap(value, axis, mask):
    return lax.ppermute(value, axis, [(i, i ^ mask) for i in range(lax.axis_size(axis))])


def expert_groups():
    groups = []
    for lat in range(4):
        for k in range(4):
            group = []
            for e in range(EXPERTS):
                place = lat ^ 2 if (e // 2) % 2 else lat
                group.append(place * 64 + 8 * (e // 2) + (7 - k if e % 2 else k))
            groups.append(group)
    return groups


def exchange(value):
    return lax.all_to_all(
        value, ("lat", "lon"), 0, 0, axis_index_groups=expert_groups(), tiled=True
    )


def on_device(
    state,
    cotangent,
    land_sea,
    regime,
    first_gain,
    second_gain,
    project_weight,
    out_weight,
    pos_bias,
    up_weight,
    down_weight,
):
    land = land_sea.T
    marked, even, odd, half = call(
        mark_kernel,
        [((ROWS, COLS, D), BF), ((REACH, COLS, D), BF), ((REACH, COLS, D), BF), ((D, UNITS), BF)],
        (state, land, up_weight, down_weight),
        fetch=4,
    )
    lat_even = pair_up(even, "lat", 0, False)
    lat_odd = pair_up(odd, "lat", 1, False)
    at_even = lax.axis_index("lat") & 1 == 0
    up = jnp.where(at_even, lat_odd, lat_even)
    down = jnp.where(at_even, lat_even, lat_odd)
    tall = jnp.concatenate([up, marked, down], axis=0)
    at_even = lax.axis_index("lon") & 1 == 0
    lon_odd = pair_up(jnp.where(at_even, tall[:, :4], tall[:, 4:]), "lon", 1, True)
    lon_even = pair_up(jnp.where(at_even, tall[:, 4:], tall[:, :4]), "lon", 0, True)

    taps, outside = tap_tables()
    bias, place, sendc, triple, gains = call(
        prepare_kernel,
        [
            ((128, 128), F32),
            ((CELLS, SLOTS), BF),
            ((SLOTS, D), BF),
            ((CELLS, 3 * D), BF),
            ((2, D), F32),
        ],
        (
            pos_bias,
            jnp.asarray(taps, BF),
            jnp.asarray(outside),
            regime.reshape(ROWS, COLS).T,
            cotangent,
            land,
            state,
            first_gain.reshape(1, D),
            second_gain.reshape(1, D),
            project_weight,
        ),
    )
    fetched = swap(half, "lon", 1)

    residual, send, known = call(
        attention_kernel,
        [((CELLS, D), BF), ((SLOTS, 2 * D), BF), ((2, D, UNITS), BF)],
        (
            state,
            lat_even,
            lat_odd,
            lon_even,
            lon_odd,
            land,
            gains,
            triple,
            project_weight,
            out_weight,
            bias,
            place,
            sendc,
            half,
            fetched,
        ),
        (pltpu.VMEM((EXT, 8, D), F32), pltpu.VMEM((EXT, 16, 128), F32)),
    )
    got = exchange(send.reshape(EXPERTS, CAP, 2 * D)).reshape(SLOTS, 2 * D)
    beyond = swap(known, "lon", 2)
    outputs, keep, give = call(
        expert_kernel,
        [((SLOTS, D), BF), ((2, 4, 2, 64, D), F32), ((2, 4, 2, 64, D), BF)],
        (
            got,
            up_weight,
            down_weight,
            fetched,
            beyond,
            swap(fetched, "lat", 1),
            swap(beyond, "lat", 1),
        ),
        (pltpu.VMEM((4, 2, 256, D), F32),),
    )
    near = swap(give, "lat", 1)
    sent = (keep[1] + near[1].astype(F32)).astype(BF)
    outputs, sent = lax.optimization_barrier((outputs, sent))
    returned = exchange(outputs.reshape(EXPERTS, CAP, D)).reshape(SLOTS, D)
    far = swap(sent, "lat", 2)
    part = keep[0] + near[0].astype(F32) + far.astype(F32)
    others = [swap(part[mask].astype(BF), "lon", mask) for mask in (1, 2, 3)]
    block, total = call(
        combine_kernel,
        [((ROWS, COLS, D), BF), ((2, 64, D), BF)],
        (returned, place, residual, land, part[0], *others),
    )
    grad_up, grad_down = call(
        gather_kernel,
        [((D, UNITS), F32), ((UNITS, D), F32)],
        (total, *[swap(total, "lat", mask) for mask in (1, 2, 3)]),
    )
    return block, grad_up, grad_down


def solution(mesh):
    placed = (
        P("lat", "lon", None),
        P("lat", "lon", None),
        P("lat", "lon"),
        P("lat", "lon", None, None, None),
        P(),
        P(),
        P(),
        P(),
        P(),
        P(None, "lon"),
        P("lon", None),
    )
    return jax.shard_map(
        on_device,
        mesh=mesh,
        in_specs=placed,
        out_specs=(P("lat", "lon", None), P(None, "lon"), P("lon", None)),
        check_vma=False,
    )
```

```python
import math

import jax
import jax.numpy as jnp
import numpy as np
from jax import lax
from jax.experimental import pallas as pl
from jax.experimental.pallas import tpu as pltpu
from jax.sharding import PartitionSpec as P

WINDOW = 7
REACH = WINDOW // 2
EXPERTS = 16
ROWS = 16
COLS = 8
CELLS = ROWS * COLS
D = 256
HEADS = 8
HD = 32
CAP = 16
SLOTS = EXPERTS * CAP
UNITS = 256
EXT = ROWS + 2 * REACH
LAND = 1024.0
FAR = -1e30
F32 = jnp.float32
BF = jnp.bfloat16
VMEM_LIMIT = 48 * 1024 * 1024


def vmem(count):
    return [pl.BlockSpec(memory_space=pltpu.VMEM)] * count


def dot(a, b):
    return lax.dot_general(a, b, (((1,), (0,)), ((), ())), preferred_element_type=F32)


def dot_t(a, b):
    return lax.dot_general(a, b, (((1,), (1,)), ((), ())), preferred_element_type=F32)


def t_dot(a, b):
    return lax.dot_general(a, b, (((0,), (0,)), ((), ())), preferred_element_type=F32)


def layer_norm(values, gain):
    mean_val = jnp.mean(values, axis=-1, keepdims=True)
    spread = jnp.mean(jnp.square(values - mean_val), axis=-1, keepdims=True)
    return ((values - mean_val) * lax.rsqrt(spread + 1e-05) * gain).astype(BF)


def tap_tables():
    column = np.concatenate([np.arange(8) + 3, np.arange(4) - 1, np.arange(4) + 11])
    table = np.zeros((WINDOW * WINDOW, 16, 8, 16), np.float32)
    for q in range(16):
        for a in range(8):
            for slot in range(16):
                da, db = a - q // 8, column[slot] - q % 8
                if 0 <= da < WINDOW and 0 <= db < WINDOW:
                    table[da * WINDOW + db, q, a, slot] = 1.0
    outside = (1.0 - table.sum(0)) * FAR
    return table.reshape(WINDOW * WINDOW, 2048), outside.reshape(1, 2048).astype(np.float32)


def column(table):
    return jnp.concatenate([table[:, i : i + 1] for i in range(ROWS)], axis=0)


def mark_kernel(state_ref, land_ref, marked_ref, even_ref, odd_ref):
    even = lax.axis_index("lat") & 1 == 0
    land = column(land_ref[...]).reshape(ROWS, COLS, 1)
    state = state_ref[...].astype(F32).reshape(ROWS, COLS, D)
    marked = jnp.where(land > 0, state, LAND).astype(BF)
    marked_ref[...] = marked
    top, bottom = marked[:REACH], marked[ROWS - REACH :]
    even_ref[...] = jnp.where(even, bottom, top)
    odd_ref[...] = jnp.where(even, top, bottom)


def half_kernel(up_ref, down_ref, half_ref):
    half_ref[...] = jnp.where(lax.axis_index("lat") & 1 == 0, up_ref[...], down_ref[...])


def prepare_kernel(
    pos_ref,
    taps_ref,
    outside_ref,
    labels_ref,
    cot_ref,
    land_ref,
    state_ref,
    gain1_ref,
    gain2_ref,
    project_ref,
    bias_ref,
    place_ref,
    sendc_ref,
    triple_ref,
    gains_ref,
):
    land = column(land_ref[...])
    gains_ref[0:1] = gain1_ref[...]
    gains_ref[1:2] = gain2_ref[...]
    own = state_ref[...].astype(F32).reshape(CELLS, D)
    triple_ref[...] = dot(layer_norm(own, gain1_ref[...]), project_ref[...]).astype(BF)
    pos = pos_ref[...]
    high = pos.astype(BF)
    rest = pos - high.astype(F32)
    middle = rest.astype(BF)
    low = (rest - middle.astype(F32)).astype(BF)
    taps = taps_ref[...]
    bias = dot(high, taps) + dot(middle, taps) + dot(low, taps) + outside_ref[...]
    for q in range(16):
        bias_ref[q * 8 : q * 8 + 8, :] = bias[:, q * 128 : q * 128 + 128]
    labels = column(labels_ref[...])
    named = lax.broadcasted_iota(jnp.int32, (CELLS, EXPERTS), 1) == labels
    named = jnp.where(named, 1.0, 0.0)
    earlier = lax.broadcasted_iota(jnp.int32, (CELLS, CELLS), 1) < lax.broadcasted_iota(
        jnp.int32, (CELLS, CELLS), 0
    )
    before = dot(jnp.where(earlier, 1.0, 0.0).astype(BF), named.astype(BF))
    rank = jnp.sum(before * named, axis=1, keepdims=True)
    slot = labels * CAP + rank.astype(jnp.int32)
    place = lax.broadcasted_iota(jnp.int32, (CELLS, SLOTS), 1) == slot
    place = jnp.where(place, 1.0, 0.0).astype(BF)
    place_ref[...] = place
    tangent = cot_ref[...].astype(F32).reshape(CELLS, D) * land.astype(F32)
    sendc_ref[...] = t_dot(place, tangent.astype(BF)).astype(BF)


def in_order(axis, even_ref, odd_ref):
    even, odd = even_ref[...].astype(F32), odd_ref[...].astype(F32)
    at_even = lax.axis_index(axis) & 1 == 0
    return jnp.where(at_even, odd, even), jnp.where(at_even, even, odd)


def attention_kernel(
    own_ref,
    lat_even_ref,
    lat_odd_ref,
    lon_even_ref,
    lon_odd_ref,
    land_ref,
    gains_ref,
    triple_ref,
    project_ref,
    out_ref,
    bias_ref,
    place_ref,
    sendc_ref,
    half_ref,
    near_ref,
    residual_ref,
    send_ref,
    fetched_ref,
    side_ref,
    pen_ref,
):
    fetched_ref[0] = half_ref[...]
    fetched_ref[1] = near_ref[...]
    lat = lax.axis_index("lat")
    top = jnp.where(lat == 0, FAR, 0.0).astype(F32)
    bottom = jnp.where(lat == lax.axis_size("lat") - 1, FAR, 0.0).astype(F32)
    up, down = in_order("lat", lat_even_ref, lat_odd_ref)
    left, right = in_order("lon", lon_even_ref, lon_odd_ref)
    side_ref[:, 0:4] = left
    side_ref[:, 4:8] = right
    side = side_ref[...]

    def marked(piece):
        return jnp.where(piece[:, :, 0:128] > 0.5 * LAND, FAR, 0.0)

    own_rows = pl.ds(REACH, ROWS)
    land = column(land_ref[...]).reshape(ROWS, COLS, 1)
    pen_ref[:, 8:16] = marked(side)
    pen_ref[0:REACH, 0:8] = marked(up)
    pen_ref[own_rows, 0:8] = jnp.broadcast_to(jnp.where(land > 0, 0.0, FAR), (ROWS, COLS, 128))
    pen_ref[REACH + ROWS : EXT, 0:8] = marked(down)
    pen_ref[0:REACH] = pen_ref[0:REACH] + top
    pen_ref[REACH + ROWS : EXT] = pen_ref[REACH + ROWS : EXT] + bottom
    pen = pen_ref[...].reshape(EXT * 16, 128).astype(BF)

    halo = jnp.concatenate([side, up, down], axis=0).reshape((EXT + 2 * REACH) * 8, D)
    halo = dot(layer_norm(halo, gains_ref[0:1]), project_ref[:, D : 3 * D])
    halo = halo.reshape(EXT + 2 * REACH, 8, 2 * D)
    middle = triple_ref[:, D : 3 * D].astype(F32).reshape(ROWS, COLS, 2 * D)
    middle = jnp.concatenate([halo[EXT : EXT + REACH], middle, halo[EXT + REACH :]], axis=0)
    keyvals = jnp.concatenate([middle, halo[:EXT]], axis=1).reshape(EXT * 16, 2 * D).astype(BF)
    queries = triple_ref[:, 0:D]
    own = own_ref[...].astype(F32).reshape(CELLS, D)

    row = lax.broadcasted_iota(jnp.int32, (128, D), 0)
    lane = lax.broadcasted_iota(jnp.int32, (128, D), 1)
    head_mask = jnp.where(lane // HD == row % HEADS, 1.0, 0.0)
    spread = jnp.where(
        lax.broadcasted_iota(jnp.int32, (128, 16), 0) // HEADS
        == lax.broadcasted_iota(jnp.int32, (128, 16), 1),
        1.0,
        0.0,
    ).astype(BF)
    gather = jnp.where(
        lax.broadcasted_iota(jnp.int32, (16, 128), 1) // HEADS
        == lax.broadcasted_iota(jnp.int32, (16, 128), 0),
        1.0,
        0.0,
    ).astype(BF)
    row = lax.broadcasted_iota(jnp.int32, (128, 128), 0)
    lane = lax.broadcasted_iota(jnp.int32, (128, 128), 1)
    first_lane = jnp.where(lane[0:8] == 0, 1.0, 0.0).astype(BF)
    query = row // HEADS
    centre = lane == (query // COLS + REACH) * 16 + query % COLS
    bias = bias_ref[...]
    scale = 1.0 / math.sqrt(HD)
    closed = dot_t(first_lane, pen)
    pairs = range(ROWS // 2)
    scores = []
    for pair in pairs:
        wide = (dot(spread, queries[16 * pair : 16 * pair + 16]) * head_mask).astype(BF)
        scores.append(dot_t(wide, keyvals[32 * pair : 32 * pair + 128, 0:D]))
    weights = []
    for pair in pairs:
        shut = jnp.concatenate([closed[:, 32 * pair : 32 * pair + 128]] * 16, axis=0)
        score = scores[pair] * scale + bias + jnp.where(centre, 0.0, shut)
        raw = jnp.exp(score - jnp.max(score, axis=1, keepdims=True))
        weights.append((raw / jnp.sum(raw, axis=1, keepdims=True)).astype(BF))
    pieces = []
    for pair in pairs:
        taken = dot(weights[pair], keyvals[32 * pair : 32 * pair + 128, D : 2 * D])
        pieces.append(dot(gather, (taken * head_mask).astype(BF)))
    attended = jnp.concatenate(pieces, axis=0).astype(BF)
    residual = (own + dot(attended, out_ref[...])).astype(BF)
    residual_ref[...] = residual
    second = layer_norm(residual.astype(F32), gains_ref[1:2])
    send_ref[:, 0:D] = t_dot(place_ref[...], second).astype(BF)
    send_ref[:, D : 2 * D] = sendc_ref[...]


def gelu_parts(hidden):
    half = 0.5 * (1.0 + lax.erf(hidden * 0.7071067811865476))
    slope = half + hidden * jnp.exp(-0.5 * hidden * hidden) * 0.3989422804014327
    return hidden * half, slope


def expert_kernel(
    got_ref,
    up_ref,
    down_ref,
    mine1_ref,
    mine2_ref,
    other1_ref,
    other2_ref,
    outputs_ref,
    keep_ref,
    give_ref,
    grad_ref,
):
    lat = lax.axis_index("lat")
    first_core = lat & 1 == 0
    inputs = got_ref[:, 0:D]
    tangents = got_ref[:, D : 2 * D]
    ups, downs = [up_ref[...]], [down_ref[...]]
    for mine, other in (
        (mine1_ref[...], other1_ref[...]),
        (mine2_ref[0], other2_ref[0]),
        (mine2_ref[1], other2_ref[1]),
    ):
        ups.append(jnp.where(first_core, mine, other))
        downs.append(jnp.where(first_core, other, mine))
    hidden = [dot(inputs, up) for up in ups]
    back = [dot_t(tangents, down) for down in downs]
    active, pre_act = [], []
    for member in range(4):
        value, slope = gelu_parts(hidden[member])
        active.append(value.astype(BF))
        pre_act.append((back[member] * slope).astype(BF))
    for member in range(4):
        grad_ref[member, 0] = t_dot(inputs, pre_act[member])
        grad_ref[member, 1] = t_dot(active[member], tangents)
    outputs = dot(active[0], downs[0])
    for member in range(1, 4):
        outputs = outputs + dot(active[member], downs[member])
    outputs_ref[...] = outputs.astype(BF)
    for far in range(2):
        for other in range(2):
            start = pl.multiple_of(jnp.bitwise_xor(lat, 2 * far + other) * 64, 64)
            chunk = grad_ref[:, :, pl.ds(start, 64), :]
            if other:
                give_ref[far] = chunk.astype(BF)
            else:
                keep_ref[far] = chunk


def combine_kernel(
    returned_ref, place_ref, residual_ref, land_ref, part_ref, a_ref, b_ref, c_ref, block_ref, total_ref
):
    rows = dot(place_ref[...], returned_ref[...])
    land = column(land_ref[...]).astype(F32)
    block_ref[...] = (
        (land * (residual_ref[...].astype(F32) + rows)).astype(BF).reshape(ROWS, COLS, D)
    )
    total = part_ref[...] + a_ref[...].astype(F32)
    total_ref[...] = (total + b_ref[...].astype(F32) + c_ref[...].astype(F32)).astype(BF)


def gather_kernel(own_ref, a_ref, b_ref, c_ref, up_ref, down_ref):
    lat = lax.axis_index("lat")
    for mask, ref in enumerate((own_ref, a_ref, b_ref, c_ref)):
        start = pl.multiple_of(jnp.bitwise_xor(lat, mask) * 64, 64)
        up_ref[pl.ds(start, 64), :] = ref[0].astype(F32)
        down_ref[pl.ds(start, 64), :] = ref[1].astype(F32)


def call(kernel, outs, args, scratch=(), fetch=0):
    def fetching(*refs):
        kept = len(args) + len(outs) + len(scratch)
        copies = [
            pltpu.make_async_copy(refs[i], refs[kept + i], refs[-1].at[i]) for i in range(fetch)
        ]
        for copy in copies:
            copy.start()
        for copy in copies:
            copy.wait()
        kernel(*refs[kept : kept + fetch], *refs[fetch:kept])

    spaces = [pltpu.HBM] * fetch + [pltpu.VMEM] * (len(args) - fetch)
    landing = [pltpu.VMEM(arg.shape, arg.dtype) for arg in args[:fetch]]
    if fetch:
        landing.append(pltpu.SemaphoreType.DMA((fetch,)))
    return pl.pallas_call(
        fetching if fetch else kernel,
        out_shape=[jax.ShapeDtypeStruct(shape, dtype) for shape, dtype in outs],
        in_specs=[pl.BlockSpec(memory_space=space) for space in spaces],
        out_specs=vmem(len(outs)),
        scratch_shapes=list(scratch) + landing,
        compiler_params=pltpu.CompilerParams(vmem_limit_bytes=None if fetch else VMEM_LIMIT),
    )(*args)


def pair_up(value, axis, first, closed):
    count = lax.axis_size(axis)
    pairs = []
    for i in range(first, count if closed else count - 1, 2):
        pairs += [(i, (i + 1) % count), ((i + 1) % count, i)]
    return lax.ppermute(value, axis, pairs)


def swap(value, axis, mask):
    return lax.ppermute(value, axis, [(i, i ^ mask) for i in range(lax.axis_size(axis))])


def expert_groups():
    groups = []
    for lat in range(4):
        for k in range(4):
            group = []
            for e in range(EXPERTS):
                place = lat ^ 2 if (e // 2) % 2 else lat
                group.append(place * 64 + 8 * (e // 2) + (7 - k if e % 2 else k))
            groups.append(group)
    return groups


def exchange(value):
    return lax.all_to_all(
        value, ("lat", "lon"), 0, 0, axis_index_groups=expert_groups(), tiled=True
    )


def on_device(
    state,
    cotangent,
    land_sea,
    regime,
    first_gain,
    second_gain,
    project_weight,
    out_weight,
    pos_bias,
    up_weight,
    down_weight,
):
    land = land_sea.T
    marked, even, odd = call(
        mark_kernel,
        [((ROWS, COLS, D), BF), ((REACH, COLS, D), BF), ((REACH, COLS, D), BF)],
        (state.reshape(CELLS, D), land),
        fetch=2,
    )
    (half,) = call(half_kernel, [((D, UNITS), BF)], (up_weight, down_weight), fetch=2)
    lat_even = pair_up(even, "lat", 0, False)
    lat_odd = pair_up(odd, "lat", 1, False)
    at_even = lax.axis_index("lat") & 1 == 0
    up = jnp.where(at_even, lat_odd, lat_even)
    down = jnp.where(at_even, lat_even, lat_odd)
    tall = jnp.concatenate([up, marked, down], axis=0)
    at_even = lax.axis_index("lon") & 1 == 0
    lon_odd = pair_up(jnp.where(at_even, tall[:, :4], tall[:, 4:]), "lon", 1, True)
    lon_even = pair_up(jnp.where(at_even, tall[:, 4:], tall[:, :4]), "lon", 0, True)

    taps, outside = tap_tables()
    bias, place, sendc, triple, gains = call(
        prepare_kernel,
        [
            ((128, 128), F32),
            ((CELLS, SLOTS), BF),
            ((SLOTS, D), BF),
            ((CELLS, 3 * D), BF),
            ((2, D), F32),
        ],
        (
            pos_bias,
            jnp.asarray(taps, BF),
            jnp.asarray(outside),
            regime.reshape(ROWS, COLS).T,
            cotangent,
            land,
            state,
            first_gain.reshape(1, D),
            second_gain.reshape(1, D),
            project_weight,
        ),
    )
    fetched = swap(half, "lon", 1)

    residual, send, known = call(
        attention_kernel,
        [((CELLS, D), BF), ((SLOTS, 2 * D), BF), ((2, D, UNITS), BF)],
        (
            state,
            lat_even,
            lat_odd,
            lon_even,
            lon_odd,
            land,
            gains,
            triple,
            project_weight,
            out_weight,
            bias,
            place,
            sendc,
            half,
            fetched,
        ),
        (pltpu.VMEM((EXT, 8, D), F32), pltpu.VMEM((EXT, 16, 128), F32)),
    )
    got = exchange(send.reshape(EXPERTS, CAP, 2 * D)).reshape(SLOTS, 2 * D)
    beyond = swap(known, "lon", 2)
    outputs, keep, give = call(
        expert_kernel,
        [((SLOTS, D), BF), ((2, 4, 2, 64, D), F32), ((2, 4, 2, 64, D), BF)],
        (
            got,
            up_weight,
            down_weight,
            fetched,
            beyond,
            swap(fetched, "lat", 1),
            swap(beyond, "lat", 1),
        ),
        (pltpu.VMEM((4, 2, 256, D), F32),),
    )
    near = swap(give, "lat", 1)
    sent = (keep[1] + near[1].astype(F32)).astype(BF)
    outputs, sent = lax.optimization_barrier((outputs, sent))
    returned = exchange(outputs.reshape(EXPERTS, CAP, D)).reshape(SLOTS, D)
    far = swap(sent, "lat", 2)
    part = keep[0] + near[0].astype(F32) + far.astype(F32)
    others = [swap(part[mask].astype(BF), "lon", mask) for mask in (1, 2, 3)]
    block, total = call(
        combine_kernel,
        [((ROWS, COLS, D), BF), ((2, 64, D), BF)],
        (returned, place, residual, land, part[0], *others),
    )
    grad_up, grad_down = call(
        gather_kernel,
        [((D, UNITS), F32), ((UNITS, D), F32)],
        (total, *[swap(total, "lat", mask) for mask in (1, 2, 3)]),
    )
    return block, grad_up, grad_down


def solution(mesh):
    placed = (
        P("lat", "lon", None),
        P("lat", "lon", None),
        P("lat", "lon"),
        P("lat", "lon", None, None, None),
        P(),
        P(),
        P(),
        P(),
        P(),
        P(None, "lon"),
        P("lon", None),
    )
    return jax.shard_map(
        on_device,
        mesh=mesh,
        in_specs=placed,
        out_specs=(P("lat", "lon", None), P(None, "lon"), P("lon", None)),
        check_vma=False,
    )
```

```python
import math

import jax
import jax.numpy as jnp
import numpy as np
from jax import lax
from jax.experimental import pallas as pl
from jax.experimental.pallas import tpu as pltpu
from jax.sharding import PartitionSpec as P

WINDOW = 7
REACH = WINDOW // 2
EXPERTS = 16
ROWS = 16
COLS = 8
CELLS = ROWS * COLS
D = 256
HEADS = 8
HD = 32
CAP = 16
SLOTS = EXPERTS * CAP
UNITS = 256
EXT = ROWS + 2 * REACH
LAND = 1024.0
FAR = -1e30
F32 = jnp.float32
BF = jnp.bfloat16
VMEM_LIMIT = 48 * 1024 * 1024


def vmem(count):
    return [pl.BlockSpec(memory_space=pltpu.VMEM)] * count


def dot(a, b):
    return lax.dot_general(a, b, (((1,), (0,)), ((), ())), preferred_element_type=F32)


def dot_t(a, b):
    return lax.dot_general(a, b, (((1,), (1,)), ((), ())), preferred_element_type=F32)


def t_dot(a, b):
    return lax.dot_general(a, b, (((0,), (0,)), ((), ())), preferred_element_type=F32)


def layer_norm(values, gain):
    mean_val = jnp.mean(values, axis=-1, keepdims=True)
    spread = jnp.mean(jnp.square(values - mean_val), axis=-1, keepdims=True)
    return ((values - mean_val) * lax.rsqrt(spread + 1e-05) * gain).astype(BF)


def tap_tables():
    column = np.concatenate([np.arange(8) + 3, np.arange(4) - 1, np.arange(4) + 11])
    table = np.zeros((WINDOW * WINDOW, 16, 8, 16), np.float32)
    for q in range(16):
        for a in range(8):
            for slot in range(16):
                da, db = a - q // 8, column[slot] - q % 8
                if 0 <= da < WINDOW and 0 <= db < WINDOW:
                    table[da * WINDOW + db, q, a, slot] = 1.0
    outside = (1.0 - table.sum(0)) * FAR
    return table.reshape(WINDOW * WINDOW, 2048), outside.reshape(1, 2048).astype(np.float32)


def column(table):
    return jnp.concatenate([table[:, i : i + 1] for i in range(ROWS)], axis=0)


def mark_kernel(state_ref, land_ref, marked_ref, even_ref, odd_ref):
    even = lax.axis_index("lat") & 1 == 0
    land = column(land_ref[...]).reshape(ROWS, COLS, 1)
    state = state_ref[...].astype(F32).reshape(ROWS, COLS, D)
    marked = jnp.where(land > 0, state, LAND).astype(BF)
    marked_ref[...] = marked
    top, bottom = marked[:REACH], marked[ROWS - REACH :]
    even_ref[...] = jnp.where(even, bottom, top)
    odd_ref[...] = jnp.where(even, top, bottom)


def half_kernel(up_ref, down_ref, half_ref):
    half_ref[...] = jnp.where(lax.axis_index("lat") & 1 == 0, up_ref[...], down_ref[...])


def prepare_kernel(
    pos_ref,
    taps_ref,
    outside_ref,
    labels_ref,
    cot_ref,
    land_ref,
    state_ref,
    gain1_ref,
    gain2_ref,
    project_ref,
    bias_ref,
    place_ref,
    sendc_ref,
    triple_ref,
    gains_ref,
):
    land = column(land_ref[...])
    gains_ref[0:1] = gain1_ref[...]
    gains_ref[1:2] = gain2_ref[...]
    own = state_ref[...].astype(F32).reshape(CELLS, D)
    triple_ref[...] = dot(layer_norm(own, gain1_ref[...]), project_ref[...]).astype(BF)
    pos = pos_ref[...]
    high = pos.astype(BF)
    rest = pos - high.astype(F32)
    middle = rest.astype(BF)
    low = (rest - middle.astype(F32)).astype(BF)
    taps = taps_ref[...]
    bias = dot(high, taps) + dot(middle, taps) + dot(low, taps) + outside_ref[...]
    for q in range(16):
        bias_ref[q * 8 : q * 8 + 8, :] = bias[:, q * 128 : q * 128 + 128]
    labels = column(labels_ref[...])
    named = lax.broadcasted_iota(jnp.int32, (CELLS, EXPERTS), 1) == labels
    named = jnp.where(named, 1.0, 0.0)
    earlier = lax.broadcasted_iota(jnp.int32, (CELLS, CELLS), 1) < lax.broadcasted_iota(
        jnp.int32, (CELLS, CELLS), 0
    )
    before = dot(jnp.where(earlier, 1.0, 0.0).astype(BF), named.astype(BF))
    rank = jnp.sum(before * named, axis=1, keepdims=True)
    slot = labels * CAP + rank.astype(jnp.int32)
    place = lax.broadcasted_iota(jnp.int32, (CELLS, SLOTS), 1) == slot
    place = jnp.where(place, 1.0, 0.0).astype(BF)
    place_ref[...] = place
    tangent = cot_ref[...].astype(F32).reshape(CELLS, D) * land.astype(F32)
    sendc_ref[...] = t_dot(place, tangent.astype(BF)).astype(BF)


def in_order(axis, even_ref, odd_ref):
    even, odd = even_ref[...].astype(F32), odd_ref[...].astype(F32)
    at_even = lax.axis_index(axis) & 1 == 0
    return jnp.where(at_even, odd, even), jnp.where(at_even, even, odd)


def attention_kernel(
    own_ref,
    lat_even_ref,
    lat_odd_ref,
    lon_even_ref,
    lon_odd_ref,
    land_ref,
    gains_ref,
    triple_ref,
    project_ref,
    out_ref,
    bias_ref,
    place_ref,
    sendc_ref,
    half_ref,
    near_ref,
    residual_ref,
    send_ref,
    fetched_ref,
    side_ref,
    pen_ref,
):
    fetched_ref[0] = half_ref[...]
    fetched_ref[1] = near_ref[...]
    lat = lax.axis_index("lat")
    top = jnp.where(lat == 0, FAR, 0.0).astype(F32)
    bottom = jnp.where(lat == lax.axis_size("lat") - 1, FAR, 0.0).astype(F32)
    up, down = in_order("lat", lat_even_ref, lat_odd_ref)
    left, right = in_order("lon", lon_even_ref, lon_odd_ref)
    side_ref[:, 0:4] = left
    side_ref[:, 4:8] = right
    side = side_ref[...]

    def marked(piece):
        return jnp.where(piece[:, :, 0:128] > 0.5 * LAND, FAR, 0.0)

    own_rows = pl.ds(REACH, ROWS)
    land = column(land_ref[...]).reshape(ROWS, COLS, 1)
    pen_ref[:, 8:16] = marked(side)
    pen_ref[0:REACH, 0:8] = marked(up)
    pen_ref[own_rows, 0:8] = jnp.broadcast_to(jnp.where(land > 0, 0.0, FAR), (ROWS, COLS, 128))
    pen_ref[REACH + ROWS : EXT, 0:8] = marked(down)
    pen_ref[0:REACH] = pen_ref[0:REACH] + top
    pen_ref[REACH + ROWS : EXT] = pen_ref[REACH + ROWS : EXT] + bottom
    pen = pen_ref[...].reshape(EXT * 16, 128).astype(BF)

    halo = jnp.concatenate([side, up, down], axis=0).reshape((EXT + 2 * REACH) * 8, D)
    halo = dot(layer_norm(halo, gains_ref[0:1]), project_ref[:, D : 3 * D])
    halo = halo.reshape(EXT + 2 * REACH, 8, 2 * D)
    middle = triple_ref[:, D : 3 * D].astype(F32).reshape(ROWS, COLS, 2 * D)
    middle = jnp.concatenate([halo[EXT : EXT + REACH], middle, halo[EXT + REACH :]], axis=0)
    keyvals = jnp.concatenate([middle, halo[:EXT]], axis=1).reshape(EXT * 16, 2 * D).astype(BF)
    queries = triple_ref[:, 0:D]
    own = own_ref[...].astype(F32).reshape(CELLS, D)

    row = lax.broadcasted_iota(jnp.int32, (128, D), 0)
    lane = lax.broadcasted_iota(jnp.int32, (128, D), 1)
    head_mask = jnp.where(lane // HD == row % HEADS, 1.0, 0.0)
    spread = jnp.where(
        lax.broadcasted_iota(jnp.int32, (128, 16), 0) // HEADS
        == lax.broadcasted_iota(jnp.int32, (128, 16), 1),
        1.0,
        0.0,
    ).astype(BF)
    gather = jnp.where(
        lax.broadcasted_iota(jnp.int32, (16, 128), 1) // HEADS
        == lax.broadcasted_iota(jnp.int32, (16, 128), 0),
        1.0,
        0.0,
    ).astype(BF)
    row = lax.broadcasted_iota(jnp.int32, (128, 128), 0)
    lane = lax.broadcasted_iota(jnp.int32, (128, 128), 1)
    first_lane = jnp.where(lane[0:8] == 0, 1.0, 0.0).astype(BF)
    query = row // HEADS
    centre = lane == (query // COLS + REACH) * 16 + query % COLS
    bias = bias_ref[...]
    scale = 1.0 / math.sqrt(HD)
    closed = dot_t(first_lane, pen)
    pairs = range(ROWS // 2)
    scores = []
    for pair in pairs:
        wide = (dot(spread, queries[16 * pair : 16 * pair + 16]) * head_mask).astype(BF)
        scores.append(dot_t(wide, keyvals[32 * pair : 32 * pair + 128, 0:D]))
    weights = []
    for pair in pairs:
        shut = jnp.concatenate([closed[:, 32 * pair : 32 * pair + 128]] * 16, axis=0)
        score = scores[pair] * scale + bias + jnp.where(centre, 0.0, shut)
        raw = jnp.exp(score - jnp.max(score, axis=1, keepdims=True))
        weights.append((raw / jnp.sum(raw, axis=1, keepdims=True)).astype(BF))
    pieces = []
    for pair in pairs:
        taken = dot(weights[pair], keyvals[32 * pair : 32 * pair + 128, D : 2 * D])
        pieces.append(dot(gather, (taken * head_mask).astype(BF)))
    attended = jnp.concatenate(pieces, axis=0).astype(BF)
    residual = (own + dot(attended, out_ref[...])).astype(BF)
    residual_ref[...] = residual
    second = layer_norm(residual.astype(F32), gains_ref[1:2])
    send_ref[:, 0:D] = t_dot(place_ref[...], second).astype(BF)
    send_ref[:, D : 2 * D] = sendc_ref[...]


def gelu_parts(hidden):
    half = 0.5 * (1.0 + lax.erf(hidden * 0.7071067811865476))
    slope = half + hidden * jnp.exp(-0.5 * hidden * hidden) * 0.3989422804014327
    return hidden * half, slope


def expert_kernel(
    got_ref,
    up_ref,
    down_ref,
    mine1_ref,
    mine2_ref,
    other1_ref,
    other2_ref,
    outputs_ref,
    keep_ref,
    give_ref,
    grad_ref,
):
    lat = lax.axis_index("lat")
    first_core = lat & 1 == 0
    inputs = got_ref[:, 0:D]
    tangents = got_ref[:, D : 2 * D]
    ups, downs = [up_ref[...]], [down_ref[...]]
    for mine, other in (
        (mine1_ref[...], other1_ref[...]),
        (mine2_ref[0], other2_ref[0]),
        (mine2_ref[1], other2_ref[1]),
    ):
        ups.append(jnp.where(first_core, mine, other))
        downs.append(jnp.where(first_core, other, mine))
    hidden = [dot(inputs, up) for up in ups]
    back = [dot_t(tangents, down) for down in downs]
    active, pre_act = [], []
    for member in range(4):
        value, slope = gelu_parts(hidden[member])
        active.append(value.astype(BF))
        pre_act.append((back[member] * slope).astype(BF))
    for member in range(4):
        grad_ref[member, 0] = t_dot(inputs, pre_act[member])
        grad_ref[member, 1] = t_dot(active[member], tangents)
    outputs = dot(active[0], downs[0])
    for member in range(1, 4):
        outputs = outputs + dot(active[member], downs[member])
    outputs_ref[...] = outputs.astype(BF)
    for far in range(2):
        for other in range(2):
            start = pl.multiple_of(jnp.bitwise_xor(lat, 2 * far + other) * 64, 64)
            chunk = grad_ref[:, :, pl.ds(start, 64), :]
            if other:
                give_ref[far] = chunk.astype(BF)
            else:
                keep_ref[far] = chunk


def total_kernel(returned_ref, part_ref, a_ref, b_ref, c_ref, total_ref):
    total = part_ref[...] + a_ref[...].astype(F32)
    total_ref[...] = (total + b_ref[...].astype(F32) + c_ref[...].astype(F32)).astype(BF)


def combine_kernel(returned_ref, place_ref, residual_ref, land_ref, block_ref):
    rows = dot(place_ref[...], returned_ref[...])
    land = column(land_ref[...]).astype(F32)
    block_ref[...] = (
        (land * (residual_ref[...].astype(F32) + rows)).astype(BF).reshape(ROWS, COLS, D)
    )


def gather_kernel(own_ref, a_ref, b_ref, c_ref, up_ref, down_ref):
    lat = lax.axis_index("lat")
    for mask, ref in enumerate((own_ref, a_ref, b_ref, c_ref)):
        start = pl.multiple_of(jnp.bitwise_xor(lat, mask) * 64, 64)
        up_ref[pl.ds(start, 64), :] = ref[0].astype(F32)
        down_ref[pl.ds(start, 64), :] = ref[1].astype(F32)


def call(kernel, outs, args, scratch=(), fetch=0):
    def fetching(*refs):
        kept = len(args) + len(outs) + len(scratch)
        copies = [
            pltpu.make_async_copy(refs[i], refs[kept + i], refs[-1].at[i]) for i in range(fetch)
        ]
        for copy in copies:
            copy.start()
        for copy in copies:
            copy.wait()
        kernel(*refs[kept : kept + fetch], *refs[fetch:kept])

    spaces = [pltpu.HBM] * fetch + [pltpu.VMEM] * (len(args) - fetch)
    landing = [pltpu.VMEM(arg.shape, arg.dtype) for arg in args[:fetch]]
    if fetch:
        landing.append(pltpu.SemaphoreType.DMA((fetch,)))
    return pl.pallas_call(
        fetching if fetch else kernel,
        out_shape=[jax.ShapeDtypeStruct(shape, dtype) for shape, dtype in outs],
        in_specs=[pl.BlockSpec(memory_space=space) for space in spaces],
        out_specs=vmem(len(outs)),
        scratch_shapes=list(scratch) + landing,
        compiler_params=pltpu.CompilerParams(vmem_limit_bytes=None if fetch else VMEM_LIMIT),
    )(*args)


def pair_up(value, axis, first, closed):
    count = lax.axis_size(axis)
    pairs = []
    for i in range(first, count if closed else count - 1, 2):
        pairs += [(i, (i + 1) % count), ((i + 1) % count, i)]
    return lax.ppermute(value, axis, pairs)


def swap(value, axis, mask):
    return lax.ppermute(value, axis, [(i, i ^ mask) for i in range(lax.axis_size(axis))])


def expert_groups():
    groups = []
    for lat in range(4):
        for k in range(4):
            group = []
            for e in range(EXPERTS):
                place = lat ^ 2 if (e // 2) % 2 else lat
                group.append(place * 64 + 8 * (e // 2) + (7 - k if e % 2 else k))
            groups.append(group)
    return groups


def exchange(value):
    return lax.all_to_all(
        value, ("lat", "lon"), 0, 0, axis_index_groups=expert_groups(), tiled=True
    )


def on_device(
    state,
    cotangent,
    land_sea,
    regime,
    first_gain,
    second_gain,
    project_weight,
    out_weight,
    pos_bias,
    up_weight,
    down_weight,
):
    land = land_sea.T
    marked, even, odd = call(
        mark_kernel,
        [((ROWS, COLS, D), BF), ((REACH, COLS, D), BF), ((REACH, COLS, D), BF)],
        (state.reshape(CELLS, D), land),
        fetch=2,
    )
    (half,) = call(half_kernel, [((D, UNITS), BF)], (up_weight, down_weight), fetch=2)
    lat_even = pair_up(even, "lat", 0, False)
    lat_odd = pair_up(odd, "lat", 1, False)
    at_even = lax.axis_index("lat") & 1 == 0
    up = jnp.where(at_even, lat_odd, lat_even)
    down = jnp.where(at_even, lat_even, lat_odd)
    tall = jnp.concatenate([up, marked, down], axis=0)
    at_even = lax.axis_index("lon") & 1 == 0
    lon_odd = pair_up(jnp.where(at_even, tall[:, :4], tall[:, 4:]), "lon", 1, True)
    lon_even = pair_up(jnp.where(at_even, tall[:, 4:], tall[:, :4]), "lon", 0, True)

    taps, outside = tap_tables()
    bias, place, sendc, triple, gains = call(
        prepare_kernel,
        [
            ((128, 128), F32),
            ((CELLS, SLOTS), BF),
            ((SLOTS, D), BF),
            ((CELLS, 3 * D), BF),
            ((2, D), F32),
        ],
        (
            pos_bias,
            jnp.asarray(taps, BF),
            jnp.asarray(outside),
            regime.reshape(ROWS, COLS).T,
            cotangent,
            land,
            state,
            first_gain.reshape(1, D),
            second_gain.reshape(1, D),
            project_weight,
        ),
    )
    fetched = swap(half, "lon", 1)

    residual, send, known = call(
        attention_kernel,
        [((CELLS, D), BF), ((SLOTS, 2 * D), BF), ((2, D, UNITS), BF)],
        (
            state,
            lat_even,
            lat_odd,
            lon_even,
            lon_odd,
            land,
            gains,
            triple,
            project_weight,
            out_weight,
            bias,
            place,
            sendc,
            half,
            fetched,
        ),
        (pltpu.VMEM((EXT, 8, D), F32), pltpu.VMEM((EXT, 16, 128), F32)),
    )
    got = exchange(send.reshape(EXPERTS, CAP, 2 * D)).reshape(SLOTS, 2 * D)
    beyond = swap(known, "lon", 2)
    outputs, keep, give = call(
        expert_kernel,
        [((SLOTS, D), BF), ((2, 4, 2, 64, D), F32), ((2, 4, 2, 64, D), BF)],
        (
            got,
            up_weight,
            down_weight,
            fetched,
            beyond,
            swap(fetched, "lat", 1),
            swap(beyond, "lat", 1),
        ),
        (pltpu.VMEM((4, 2, 256, D), F32),),
    )
    near = swap(give, "lat", 1)
    sent = (keep[1] + near[1].astype(F32)).astype(BF)
    outputs, sent = lax.optimization_barrier((outputs, sent))
    returned = exchange(outputs.reshape(EXPERTS, CAP, D)).reshape(SLOTS, D)
    far = swap(sent, "lat", 2)
    part = keep[0] + near[0].astype(F32) + far.astype(F32)
    others = [swap(part[mask].astype(BF), "lon", mask) for mask in (1, 2, 3)]
    (total,) = call(total_kernel, [((2, 64, D), BF)], (returned, part[0], *others))
    (block,) = call(
        combine_kernel, [((ROWS, COLS, D), BF)], (returned, place, residual, land)
    )
    grad_up, grad_down = call(
        gather_kernel,
        [((D, UNITS), F32), ((UNITS, D), F32)],
        (total, *[swap(total, "lat", mask) for mask in (1, 2, 3)]),
    )
    return block, grad_up, grad_down


def solution(mesh):
    placed = (
        P("lat", "lon", None),
        P("lat", "lon", None),
        P("lat", "lon"),
        P("lat", "lon", None, None, None),
        P(),
        P(),
        P(),
        P(),
        P(),
        P(None, "lon"),
        P("lon", None),
    )
    return jax.shard_map(
        on_device,
        mesh=mesh,
        in_specs=placed,
        out_specs=(P("lat", "lon", None), P(None, "lon"), P("lon", None)),
        check_vma=False,
    )
```
